256 devices in a mesh: seq: 32 (over z_hi, y, core), res: 8 (over x, z_lo).
Axes of the slice: x: 4, y: 4, z: 8 (z_hi: 4, z_lo: 2; z = z_hi * 2 + z_lo), core: 2. Of those that a mesh axis runs over, the one named last changes fastest.
Arguments:
- alignment_embeddings: bfloat16 [128, 1024, 768], P('seq', 'res'), may hold values from -10 to 10
- query_matrix: bfloat16 [768, 768], replicated, may hold values from -0.21875 to 0.21875
- key_matrix: bfloat16 [768, 768], replicated, may hold values from -0.21875 to 0.21875
- value_matrix: bfloat16 [768, 768], replicated, may hold values from -0.21875 to 0.21875
- output_matrix: bfloat16 [768, 768], replicated, may hold values from -0.21875 to 0.21875
Outputs:
- updated: bfloat16 [128, 1024, 768], P('seq', 'res')
The draws below stay inside these ranges and needn't reach their ends.
All inputs are finite; a program needn't handle non-finite values.
Results may differ from the reference program's by a relative error of at most 0.0076.
Values may be sent and summed in bfloat16 or wider, within the bound.
No kernel may reach another device: no remote copies, remote signals or barrier semaphores. Data moves between devices by JAX's collectives and lax.ppermute only.
A program may use at most 64 MiB of HBM per device.

```python
import jax
import jax.numpy as jnp
from jax import lax

MODEL_WIDTH = 768
HEADS = 12
HEAD = 64
SEQUENCE_COUNT = 128
RESIDUE_COUNT = 1024


def draw_alignment_embeddings(key, part):
    key = jax.random.fold_in(key, 11)
    key_base = jax.random.fold_in(key, 0)
    array_extent = (SEQUENCE_COUNT, RESIDUE_COUNT, MODEL_WIDTH)
    data = jnp.clip(jax.random.normal(key_base, array_extent, jnp.float32), -6.0, 6.0)
    return data.astype(jnp.bfloat16)


def scatter_about(key, dims, width, limit, dtype=jnp.bfloat16):
    entries = jax.random.normal(key, dims, jnp.float32) * width
    return jnp.minimum(jnp.maximum(entries, -limit), limit).astype(dtype)


def setup_inputs(seed: int = 0) -> dict:
    splits = jax.random.split(jax.random.key(seed), 6)
    return {
        "alignment_embeddings": draw_alignment_embeddings(jax.random.fold_in(splits[5], 71), 0),
        "query_matrix": scatter_about(splits[1], (MODEL_WIDTH, MODEL_WIDTH), MODEL_WIDTH ** -0.5, 0.21875),
        "key_matrix": scatter_about(splits[2], (MODEL_WIDTH, MODEL_WIDTH), MODEL_WIDTH ** -0.5, 0.21875),
        "value_matrix": scatter_about(splits[3], (MODEL_WIDTH, MODEL_WIDTH), MODEL_WIDTH ** -0.5, 0.21875),
        "output_matrix": scatter_about(splits[4], (MODEL_WIDTH, MODEL_WIDTH), MODEL_WIDTH ** -0.5, 0.21875),
    }


def reference(alignment_embeddings, query_matrix, key_matrix, value_matrix, output_matrix):
    flattened_rows = alignment_embeddings.reshape(SEQUENCE_COUNT * RESIDUE_COUNT, MODEL_WIDTH)
    scale = HEAD ** (-0.5) / jnp.sqrt(jnp.float32(SEQUENCE_COUNT))

    def head_columns(weight):
        return weight.reshape(MODEL_WIDTH, HEADS, HEAD).transpose(1, 0, 2)

    def project_head(columns):
        result = jnp.dot(flattened_rows, columns, preferred_element_type=jnp.float32).astype(jnp.bfloat16)
        return result.reshape(SEQUENCE_COUNT, RESIDUE_COUNT, HEAD)

    def one_head(carried, operands):
        query_cols, key_cols, value_cols, output_rows = operands
        query_h = project_head(query_cols)
        key_h = project_head(key_cols)
        value_h = project_head(value_cols)
        logits = jnp.einsum('rid,rjd->ij', query_h.astype(jnp.float32), key_h.astype(jnp.float32))
        scaled = logits * scale
        shifted = scaled - lax.optimization_barrier(jnp.max(scaled, axis=1, keepdims=True))
        expo = jnp.exp(shifted)
        probs = (expo / lax.optimization_barrier(jnp.sum(expo, axis=1, keepdims=True))).astype(jnp.bfloat16)
        mixed = jnp.einsum('ij,rjd->rid', probs.astype(jnp.float32), value_h.astype(jnp.float32))
        mixed = mixed.astype(jnp.bfloat16).reshape(SEQUENCE_COUNT * RESIDUE_COUNT, HEAD)
        carried = carried + jnp.dot(mixed, output_rows, preferred_element_type=jnp.float32)
        return (carried, jnp.zeros((), jnp.float32))
    start = jnp.zeros((SEQUENCE_COUNT * RESIDUE_COUNT, MODEL_WIDTH), jnp.float32)
    operands = (head_columns(query_matrix), head_columns(key_matrix), head_columns(value_matrix), output_matrix.reshape(HEADS, HEAD, MODEL_WIDTH))
    summed, unused = lax.scan(one_head, start, operands)
    return summed.astype(jnp.bfloat16).reshape(SEQUENCE_COUNT, RESIDUE_COUNT, MODEL_WIDTH)
```

```python
import jax
import jax.numpy as jnp
from jax import lax
from jax.sharding import Mesh, PartitionSpec as P

HEADS = 12
HEAD = 64
AXES = ("z_hi", "y", "core", "x", "z_lo")
SIZES = (4, 4, 2, 4, 2)
SIZE = dict(zip(AXES, SIZES))


def shift(arr, axis, step):
    n = SIZE[axis]
    return lax.ppermute(arr, axis, [(i, (i + step) % n) for i in range(n)])


def shift_z(arr, step, flip):
    pairs = [
        (hi * 2 + lo, (hi + step) % 4 * 2 + (lo ^ flip))
        for hi in range(4)
        for lo in range(2)
    ]
    return lax.ppermute(arr, ("z_hi", "z_lo"), pairs)


def pick(arr, index, axis):
    return lax.dynamic_index_in_dim(arr, index % arr.shape[axis], axis, keepdims=False)


def both_cores(arr):
    return jnp.stack([arr, shift(arr, "core", 1)])


def x_ring(arr):
    half = arr.shape[0] // 2
    below, above = shift(arr, "x", 1), shift(arr, "x", -1)
    far = jnp.concatenate([shift(below[:half], "x", 1), shift(above[half:], "x", -1)])
    return [arr, below, above, far]


def place(parts, me, axis):
    n = len(parts)
    out = jnp.zeros(parts[0].shape[:axis] + (n,) + parts[0].shape[axis:], parts[0].dtype)
    for d, part in enumerate(parts):
        out = lax.dynamic_update_index_in_dim(out, part, (me - d) % n, axis)
    return out


def per_device(data, query_matrix, key_matrix, value_matrix, output_matrix):
    seqs, rows, width = data.shape
    core, y, z_hi = (lax.axis_index(a) for a in ("core", "y", "z_hi"))
    own = width // 2
    heads = HEADS // 2

    def columns(weight):
        return lax.dynamic_slice_in_dim(weight, core * own, own, 1)

    query_matrix, key_matrix, value_matrix = map(
        columns, (query_matrix, key_matrix, value_matrix)
    )
    output_matrix = jnp.concatenate(
        [
            lax.dynamic_slice_in_dim(output_matrix, c * own, own, 0)
            for c in (core, 1 - core)
        ]
    )

    def project(block, weight):
        out = jnp.einsum("crif,fg->crig", block, weight, preferred_element_type=jnp.float32)
        return out.astype(jnp.bfloat16).reshape(*block.shape[:-1], heads, -1)

    partner = shift(data, "z_lo", 1)
    near = x_ring(data)
    near2 = [both_cores(b) for b in near]
    partner2 = both_cores(partner)
    queries = jnp.stack([project(b, query_matrix) for b in (near2[0], partner2)])
    keys = jnp.stack([project(b, key_matrix) for b in near2])
    logits = jnp.einsum(
        "acrihd,bcrjhd->ahibj", queries, keys, preferred_element_type=jnp.float32
    )
    half_cols = 4 * rows
    logits = logits.reshape(2, heads, 4, rows // 4, half_cols)
    sent = logits.astype(jnp.bfloat16)
    total = pick(logits, y, 2)
    for d in (1, 2, 3):
        total += shift(pick(sent, y + d, 2), "y", d).astype(jnp.float32)
    total = total.reshape(2, 4, heads * rows // 16, half_cols)
    sent = total.astype(jnp.bfloat16)
    sides = []
    for flip in (0, 1):
        side = pick(total[0], z_hi, 0) if flip == 0 else None
        for d in range(4):
            if flip == 0 and d == 0:
                continue
            part = shift_z(pick(sent[flip], z_hi + d, 0), d, flip).astype(jnp.float32)
            side = part if side is None else side + part
        sides.append(side)
    full = jnp.concatenate(sides, axis=1)
    all_rows = seqs * lax.axis_size(("z_hi", "y", "core"))
    scaled = full * (HEAD ** (-0.5) / jnp.sqrt(jnp.float32(all_rows)))
    expo = jnp.exp(scaled - jnp.max(scaled, axis=-1, keepdims=True))
    probs = (expo / jnp.sum(expo, axis=-1, keepdims=True)).astype(jnp.bfloat16)

    probs = place([probs] + [shift(probs, "z_hi", d) for d in (1, 2, 3)], z_hi, 0)
    probs = probs.reshape(heads, rows // 4, 2 * half_cols)
    probs = place([probs] + [shift(probs, "y", d) for d in (1, 2, 3)], y, 1)
    probs = probs.reshape(heads, rows, 8, rows)

    far2 = [partner2] + [both_cores(b) for b in x_ring(partner)[1:]]
    values = jnp.stack([project(b, value_matrix) for b in near2 + far2])
    mixed = jnp.einsum("hibj,bcrjhd->crihd", probs, values, preferred_element_type=jnp.float32)
    attended = mixed.astype(jnp.bfloat16).reshape(2, seqs, rows, own)
    attended = jnp.concatenate([attended[0], shift(attended[1], "core", 1)], axis=-1)
    return jnp.einsum(
        "rif,fg->rig", attended, output_matrix, preferred_element_type=jnp.float32
    ).astype(jnp.bfloat16)


def solution(mesh):
    fine = Mesh(mesh.devices.reshape(SIZES), AXES)
    spec = P(("z_hi", "y", "core"), ("x", "z_lo"), None)
    return jax.shard_map(
        per_device,
        mesh=fine,
        in_specs=(spec, P(), P(), P(), P()),
        out_specs=spec,
        check_vma=False,
    )
```

```python
import functools

import jax
import jax.numpy as jnp
from jax import lax
from jax.experimental import pallas as pl
from jax.experimental.pallas import tpu as pltpu
from jax.sharding import Mesh, PartitionSpec as P

HEADS = 12
HEAD = 64
AXES = ("z_hi", "y", "core", "x", "z_lo")
SIZES = (4, 4, 2, 4, 2)
SIZE = dict(zip(AXES, SIZES))
BF16 = jnp.bfloat16
F32 = jnp.float32
PARTS = 4
VMEM = 24 << 20


def shift(arr, axis, step):
    n = SIZE[axis]
    return lax.ppermute(arr, axis, [(i, (i + step) % n) for i in range(n)])


def whole(shape):
    return pl.BlockSpec(shape, lambda *_: (0,) * len(shape))


def call(body, place, ins, in_specs, outs, out_specs, grid, flops, name, late=()):
    moved = sum(a.size * a.dtype.itemsize for a in ins)
    moved += sum(o.size * o.dtype.itemsize for o in outs)
    n = 1 + len(ins)

    def run(*refs):
        body(*refs[:n], *refs[n + len(late) :])

    in_specs = [*in_specs] + [pl.BlockSpec(memory_space=pl.ANY)] * len(late)
    return pl.pallas_call(
        run,
        out_shape=outs,
        grid_spec=pltpu.PrefetchScalarGridSpec(
            num_scalar_prefetch=1, grid=grid, in_specs=in_specs, out_specs=out_specs
        ),
        compiler_params=pltpu.CompilerParams(vmem_limit_bytes=VMEM),
        cost_estimate=pl.CostEstimate(flops=flops, bytes_accessed=moved, transcendentals=0),
        name=name,
    )(place, *ins, *late)


def tie(arrays, late):
    n = len(arrays)
    free = pl.BlockSpec(memory_space=pl.ANY)
    return pl.pallas_call(
        lambda *refs: None,
        out_shape=[jax.ShapeDtypeStruct(a.shape, a.dtype) for a in arrays],
        in_specs=[free] * (n + 1),
        out_specs=[free] * n,
        input_output_aliases={i: i for i in range(n)},
        name="tie",
    )(*arrays, late)


def rel(index):
    return lax.rem(index + PARTS, PARTS)


def project_body(kinds, blocks, place, *refs):
    xs = refs[: 2 * blocks]
    weights = refs[2 * blocks : 2 * blocks + len(kinds)]
    outs = refs[2 * blocks + len(kinds) :]
    y = place[1]
    seqs, rows, width = xs[0].shape
    lanes = 2 * HEAD
    pairs = weights[0].shape[1] // lanes
    group = rows // PARTS
    for b in range(blocks):
        for half in range(2):
            x = xs[2 * b + half][...].reshape(seqs * rows, width)
            for kind, weight, out in zip(kinds, weights, outs):
                got = jnp.dot(x, weight[...], preferred_element_type=F32).astype(BF16)
                for s in range(seqs):
                    at = (half * seqs + s) * lanes
                    for p in range(pairs):
                        part = got[s * rows : (s + 1) * rows, p * lanes : (p + 1) * lanes]
                        if kind != "q":
                            out[p, b * rows : (b + 1) * rows, at : at + lanes] = part
                            continue
                        first = lax.broadcasted_iota(jnp.int32, part.shape, 1) < HEAD
                        for h in range(2):
                            kept = jnp.where(first == (h == 0), part, jnp.zeros_like(part))
                            for a in range(PARTS):
                                out[p, rel(a - y), h, :, at : at + lanes] = kept[
                                    a * group : (a + 1) * group
                                ]


def project(place, blocks, weights, kinds, name, late=()):
    seqs, rows, width = blocks[0][0].shape
    own = width // 2
    pairs, span = HEADS // 4, 2 * seqs * 2 * HEAD
    ins = [a for block in blocks for a in block] + list(weights)
    in_specs = [whole((seqs, rows, width))] * (2 * len(blocks))
    in_specs += [pl.BlockSpec((width, own), lambda i, s: (0, s[0]))] * len(weights)
    shapes = [
        (pairs, PARTS, 2, rows // PARTS, span)
        if k == "q"
        else (pairs, rows * len(blocks), span)
        for k in kinds
    ]
    flops = 2 * len(blocks) * 2 * seqs * rows * width * own * len(kinds)
    return call(
        functools.partial(project_body, kinds, len(blocks)),
        place,
        ins,
        in_specs,
        [jax.ShapeDtypeStruct(s, BF16) for s in shapes],
        [whole(s) for s in shapes],
        (1,),
        flops,
        name,
        late,
    )


def logits_body(blocks, place, *refs):
    queries, keys, outs = refs[:2], refs[2 : 2 + blocks], refs[2 + blocks :]
    half = outs[0].shape[2]
    k = jnp.concatenate([ref[0] for ref in keys], axis=0)
    for i, ref in enumerate(queries):
        q = ref[0].reshape(PARTS * half, -1)
        got = lax.dot_general(q, k, (((1,), (1,)), ((), ())), preferred_element_type=F32)
        for d, out in enumerate(outs):
            out[i, 0] = got[d * half : (d + 1) * half].astype(BF16)


def make_logits(place, queries, keys, name):
    pairs, _, _, group, span = queries[0].shape
    rows = sum(k.shape[1] for k in keys)
    half = 2 * group
    shape = jax.ShapeDtypeStruct((2, pairs, half, rows), BF16)
    return call(
        functools.partial(logits_body, len(keys)),
        place,
        [*queries, *keys],
        [pl.BlockSpec((1, PARTS, 2, group, span), lambda p, s: (p, 0, 0, 0, 0))] * 2
        + [pl.BlockSpec((1, k.shape[1], span), lambda p, s: (p, 0, 0)) for k in keys],
        [shape] * PARTS,
        [pl.BlockSpec((2, 1, half, rows), lambda p, s: (0, p, 0, 0))] * PARTS,
        (pairs,),
        2 * pairs * 2 * PARTS * half * span * rows,
        name,
    )


def add_body(count, place, *refs):
    out, parts = refs[-1], refs[:-1]
    z_lo = place[3]
    sums = []
    for n in range(0, len(parts), count):
        total = parts[n][...].astype(F32)
        for ref in parts[n + 1 : n + count]:
            total += ref[...].astype(F32)
        sums.append(total)
    total = jnp.concatenate(sums, axis=-1).astype(BF16)
    share = out.shape[2]
    for i in range(2):
        for z in range(PARTS):
            out[z, i ^ z_lo] = total[i, z * share : (z + 1) * share]


def add_parts(place, groups):
    parts = [a for g in groups for a in g]
    rows = parts[0].shape[1]
    cols = sum(g[0].shape[2] for g in groups)
    shape = (PARTS, 2, rows // PARTS, cols)
    return call(
        functools.partial(add_body, PARTS),
        place,
        parts,
        [whole(a.shape) for a in parts],
        [jax.ShapeDtypeStruct(shape, BF16)],
        [whole(shape)],
        (1,),
        sum(a.size for a in parts),
        "add_over_y",
    )[0]


def softmax_body(scale, place, parts, out):
    z_lo = place[3]
    sides = []
    for side in (z_lo, 1 - z_lo):
        total = parts[0, side].astype(F32)
        for z in range(1, PARTS):
            total += parts[z, side].astype(F32)
        sides.append(total)
    scaled = jnp.concatenate(sides, axis=-1) * scale
    expo = jnp.exp(scaled - jnp.max(scaled, axis=-1, keepdims=True))
    out[...] = (expo / jnp.sum(expo, axis=-1, keepdims=True)).astype(BF16)


def softmax(place, parts, scale):
    shape = (parts.shape[2], 2 * parts.shape[3])
    return call(
        functools.partial(softmax_body, scale),
        place,
        [parts],
        [whole(parts.shape)],
        [jax.ShapeDtypeStruct(shape, BF16)],
        [whole(shape)],
        (1,),
        parts.size * 8,
        "softmax",
    )[0]


def order_body(place, *refs):
    out, parts = refs[-1], refs[:-1]
    for d, ref in enumerate(parts):
        out[rel(place[2] - d)] = ref[...]


def order(place, parts):
    shape = (PARTS, *parts[0].shape)
    return call(
        order_body,
        place,
        parts,
        [whole(a.shape) for a in parts],
        [jax.ShapeDtypeStruct(shape, BF16)],
        [whole(shape)],
        (1,),
        0,
        "order",
    )[0]


def mix_body(place, *refs):
    probs, values, outs = refs[:PARTS], refs[PARTS:-2], refs[-2:]
    y = place[1]
    group = probs[0].shape[1] // 2
    lanes = 2 * HEAD
    seqs = outs[0].shape[0]
    p = jnp.concatenate([ref[0] for ref in probs], axis=0)
    v = jnp.concatenate([ref[0] for ref in values], axis=0)
    got = jnp.dot(p, v, preferred_element_type=F32)
    first = lax.broadcasted_iota(jnp.int32, (group, lanes), 1) < HEAD
    for d in range(PARTS):
        at = pl.multiple_of(rel(y - d) * group, group)
        for s in range(2 * seqs):
            one, two = (
                got[(2 * d + h) * group : (2 * d + h + 1) * group, s * lanes : (s + 1) * lanes]
                for h in range(2)
            )
            outs[s // seqs][s % seqs, pl.ds(at, group), :] = jnp.where(first, one, two).astype(BF16)


def mix(place, probs, values, seqs):
    pairs, half, cols = probs[0].shape
    span = values[0].shape[2]
    rows = PARTS * half // 2
    lanes = 2 * HEAD
    shape = jax.ShapeDtypeStruct((seqs, rows, pairs * lanes), BF16)
    return call(
        mix_body,
        place,
        [*probs, *values],
        [pl.BlockSpec((1, half, cols), lambda p, s: (p, 0, 0))] * PARTS
        + [pl.BlockSpec((1, v.shape[1], span), lambda p, s: (p, 0, 0)) for v in values],
        [shape] * 2,
        [pl.BlockSpec((seqs, rows, lanes), lambda p, s: (0, 0, p))] * 2,
        (pairs,),
        2 * pairs * PARTS * half * cols * span,
        "mix",
    )


def finish_body(place, mine, theirs, weight_mine, weight_theirs, out):
    seqs, rows, own = mine.shape
    got = jnp.dot(mine[...].reshape(seqs * rows, own), weight_mine[...], preferred_element_type=F32)
    got += jnp.dot(
        theirs[...].reshape(seqs * rows, own), weight_theirs[...], preferred_element_type=F32
    )
    out[...] = got.astype(BF16).reshape(out.shape)


def finish(place, mine, theirs, weight):
    seqs, rows, own = mine.shape
    width = weight.shape[1]
    return call(
        finish_body,
        place,
        [mine, theirs, weight, weight],
        [pl.BlockSpec((1, rows, own), lambda r, s: (r, 0, 0))] * 2
        + [
            pl.BlockSpec((own, width), lambda r, s: (s[0], 0)),
            pl.BlockSpec((own, width), lambda r, s: (1 - s[0], 0)),
        ],
        [jax.ShapeDtypeStruct((seqs, rows, width), BF16)],
        [pl.BlockSpec((1, rows, width), lambda r, s: (r, 0, 0))],
        (seqs,),
        2 * seqs * rows * width * width,
        "finish",
    )[0]


def ring_table(axis_of):
    return [
        (c * SIZE["x"] + i, c * SIZE["x"] + (i + (1 if c == axis_of else -1)) % SIZE["x"])
        for c in range(2)
        for i in range(SIZE["x"])
    ]


def send_x(arr, way):
    return lax.ppermute(arr, ("core", "x"), ring_table(way))


def per_device(data, query_matrix, key_matrix, value_matrix, output_matrix):
    seqs, rows, width = data.shape
    place = jnp.stack([lax.axis_index(a) for a in ("core", "y", "z_hi", "z_lo")])
    place = place.astype(jnp.int32)

    def swap(arr):
        return shift(arr, "core", 1)

    first, second = send_x(data, 0), send_x(data, 1)
    partner = shift(data, "z_lo", 1)
    own = (data, swap(data))
    queries, keys, values = project(
        place, [own], [query_matrix, key_matrix, value_matrix], "qkv", "project_own"
    )
    first, second, partner = tie([first, second, partner], queries)
    far = send_x(first, 0)
    near = [(first, swap(second)), (second, swap(first))]
    partner2 = (partner, swap(partner))
    (partner_queries,) = project(place, [partner2], [query_matrix], "q", "project_partner")
    (near_keys,) = project(place, near, [key_matrix], "k", "project_near")
    both = [queries, partner_queries]
    near_logits = make_logits(place, both, [keys, near_keys], "logits_near")
    (far,) = tie([far], near_logits[0])
    far2 = (far, swap(far))
    (far_keys,) = project(place, [far2], [key_matrix], "k", "project_far")
    far_logits = make_logits(place, both, [far_keys], "logits_far")

    def over_y(parts):
        parts = [a.reshape(2, -1, a.shape[-1]) for a in parts]
        return [parts[0]] + [shift(parts[d], "y", d) for d in range(1, PARTS)]

    groups = [over_y(near_logits), over_y(far_logits)]
    (z_own,) = project(place, [partner2], [value_matrix], "v", "values_partner", far_logits[:1])
    sent = add_parts(place, groups)
    (near_values,) = project(place, [*near, far2], [value_matrix], "v", "values_near", [sent])
    (z_sent,) = tie([z_own], sent)
    z_first, z_second = send_x(z_sent, 0), send_x(z_sent, 1)

    sent = sent.reshape(2 * PARTS, *sent.shape[2:])
    got = lax.all_to_all(sent, ("z_hi", "z_lo"), 0, 0, tiled=True)
    got = got.reshape(PARTS, 2, *got.shape[1:])
    all_rows = seqs * lax.axis_size(("z_hi", "y", "core"))
    probs = softmax(place, got, HEAD ** (-0.5) * all_rows ** (-0.5))
    (z_first,) = tie([z_first], probs)
    z_far = send_x(z_first, 0)
    z_values = [z_sent, z_first, z_second, z_far]
    probs = order(place, [probs] + [shift(probs, "z_hi", d) for d in range(1, PARTS)])
    probs = probs.reshape(HEADS // 4, 2 * rows // PARTS, probs.shape[-1])
    probs = [probs] + [shift(probs, "y", d) for d in range(1, PARTS)]
    mine, theirs = mix(place, probs, [values, near_values, *z_values], seqs)
    return finish(place, mine, swap(theirs), output_matrix)


def solution(mesh):
    fine = Mesh(mesh.devices.reshape(SIZES), AXES)
    spec = P(("z_hi", "y", "core"), ("x", "z_lo"), None)
    return jax.shard_map(
        per_device,
        mesh=fine,
        in_specs=(spec, P(), P(), P(), P()),
        out_specs=spec,
        check_vma=False,
    )
```

```python
import functools

import jax
import jax.numpy as jnp
from jax import lax
from jax.experimental import pallas as pl
from jax.experimental.pallas import tpu as pltpu
from jax.sharding import Mesh, PartitionSpec as P

HEADS = 12
HEAD = 64
AXES = ("z_hi", "y", "core", "x", "z_lo")
SIZES = (4, 4, 2, 4, 2)
SIZE = dict(zip(AXES, SIZES))
BF16 = jnp.bfloat16
F32 = jnp.float32
PARTS = 4
VMEM = 16 << 20


def shift(arr, axis, step):
    n = SIZE[axis]
    return lax.ppermute(arr, axis, [(i, (i + step) % n) for i in range(n)])


def whole(shape):
    return pl.BlockSpec(shape, lambda *_: (0,) * len(shape), pipeline_mode=pl.Buffered(1))


def call(body, place, ins, in_specs, outs, out_specs, grid, flops, name, late=()):
    moved = sum(a.size * a.dtype.itemsize for a in ins)
    moved += sum(o.size * o.dtype.itemsize for o in outs)
    n = 1 + len(ins)

    def run(*refs):
        body(*refs[:n], *refs[n + len(late) :])

    in_specs = [*in_specs] + [pl.BlockSpec(memory_space=pl.ANY)] * len(late)
    return pl.pallas_call(
        run,
        out_shape=outs,
        grid_spec=pltpu.PrefetchScalarGridSpec(
            num_scalar_prefetch=1, grid=grid, in_specs=in_specs, out_specs=out_specs
        ),
        compiler_params=pltpu.CompilerParams(vmem_limit_bytes=VMEM),
        cost_estimate=pl.CostEstimate(flops=flops, bytes_accessed=moved, transcendentals=0),
        name=name,
    )(place, *ins, *late)


def tie(arrays, late):
    n = len(arrays)
    free = pl.BlockSpec(memory_space=pl.ANY)
    return pl.pallas_call(
        lambda *refs: None,
        out_shape=[jax.ShapeDtypeStruct(a.shape, a.dtype) for a in arrays],
        in_specs=[free] * (n + 1),
        out_specs=[free] * n,
        input_output_aliases={i: i for i in range(n)},
        compiler_params=pltpu.CompilerParams(vmem_limit_bytes=1 << 20),
        name="tie",
    )(*arrays, late)


def rel(index):
    return lax.rem(index + PARTS, PARTS)


def manual(body, place, ins, outs, scratch, flops, name, late=()):
    moved = sum(a.size * a.dtype.itemsize for a in ins)
    moved += sum(o.size * o.dtype.itemsize for o in outs)
    n = 1 + len(ins)
    far_off = pl.BlockSpec(memory_space=pltpu.HBM)

    def run(*refs):
        body(*refs[:n], *refs[n + len(late) :])

    return pl.pallas_call(
        run,
        out_shape=outs,
        in_specs=[pl.BlockSpec(memory_space=pltpu.SMEM)] + [far_off] * (len(ins) + len(late)),
        out_specs=[far_off] * len(outs),
        scratch_shapes=scratch,
        compiler_params=pltpu.CompilerParams(vmem_limit_bytes=VMEM),
        cost_estimate=pl.CostEstimate(flops=flops, bytes_accessed=moved, transcendentals=0),
        name=name,
    )(place, *ins, *late)


def start(src, dst, sem):
    copy = pltpu.make_async_copy(src, dst, sem)
    copy.start()
    return copy


def columns(weight, place):
    own = weight.shape[1] // 2
    return weight.at[:, pl.ds(pl.multiple_of(place[0] * own, own), own)]


def project(x_ref, half, weight, kind, out, place, base=0):
    seqs, rows, width = x_ref.shape
    lanes = 2 * HEAD
    pairs = weight.shape[1] // lanes
    group = rows // PARTS
    x = x_ref[...].reshape(seqs * rows, width)
    got = jnp.dot(x, weight[...], preferred_element_type=F32).astype(BF16)
    for s in range(seqs):
        at = (half * seqs + s) * lanes
        for p in range(pairs):
            part = got[s * rows : (s + 1) * rows, p * lanes : (p + 1) * lanes]
            if kind != "q":
                out[p, base : base + rows, at : at + lanes] = part
                continue
            first = lax.broadcasted_iota(jnp.int32, part.shape, 1) < HEAD
            for h in range(2):
                kept = jnp.where(first == (h == 0), part, jnp.zeros_like(part))
                for a in range(PARTS):
                    out[p, rel(a - place[1]), h, :, at : at + lanes] = kept[
                        a * group : (a + 1) * group
                    ]


def write_logits(queries, keys, held, outs, sems):
    half = held.shape[3]
    copies = []
    for p in range(keys.shape[0]):
        k = keys[p]
        for i, ref in enumerate(queries):
            q = ref[p].reshape(PARTS * half, -1)
            got = lax.dot_general(q, k, (((1,), (1,)), ((), ())), preferred_element_type=F32)
            for d in range(PARTS):
                held[d, i, p] = got[d * half : (d + 1) * half].astype(BF16)
        for d, out in enumerate(outs):
            copies.append(start(held.at[d, :, p], out.at[:, p], sems.at[p, d]))
    return copies


def wait_all(copies):
    for copy in copies:
        copy.wait()


def own_body(place, x0, x1, wq, wk, wv, oq, ok, ov, bx, bw, bq, bk, bv, ins, outs):
    loads = [start(x, bx.at[i], ins.at[i]) for i, x in enumerate((x0, x1))]
    loads += [start(columns(w, place), bw.at[i], ins.at[2 + i]) for i, w in enumerate((wq, wk, wv))]
    stores = []
    for i, (kind, out, held) in enumerate((("q", oq, bq), ("k", ok, bk), ("v", ov, bv))):
        loads[2 + i].wait()
        for half in range(2):
            if i == 0:
                loads[half].wait()
            project(bx.at[half], half, bw.at[i], kind, held, place)
        stores.append(start(held, out, outs.at[i]))
    wait_all(stores)


def near_body(place, q0, k0, *refs):
    xs, (wq, wk, oq), ls = refs[:6], refs[6:9], refs[9:13]
    bx, bw, bq, bk, held, ins, outs, sems = refs[13:]
    rows = k0.shape[1]
    q_in = start(q0, bq.at[0], ins.at[8])
    k_in = start(k0, bk.at[:, pl.ds(0, rows), :], ins.at[9])
    w_in = [start(columns(w, place), bw.at[i], ins.at[6 + i]) for i, w in enumerate((wq, wk))]
    x_in = [start(x, bx.at[i], ins.at[i]) for i, x in enumerate(xs)]
    w_in[0].wait()
    for half in range(2):
        x_in[half].wait()
        project(bx.at[half], half, bw.at[0], "q", bq.at[1], place)
    stored = start(bq.at[1], oq, outs.at[0])
    w_in[1].wait()
    for i in range(2, 6):
        x_in[i].wait()
        project(bx.at[i], i % 2, bw.at[1], "k", bk, place, i // 2 * rows)
    q_in.wait()
    k_in.wait()
    wait_all(write_logits([bq.at[0], bq.at[1]], bk, held, ls, sems))
    stored.wait()


def far_body(place, q0, q1, x0, x1, wk, *refs):
    ls, (bx, bw, bq, bk, held, ins, sems) = refs[:PARTS], refs[PARTS:]
    w_in = start(columns(wk, place), bw, ins.at[0])
    x_in = [start(x, bx.at[i], ins.at[1 + i]) for i, x in enumerate((x0, x1))]
    q_in = [start(q, bq.at[i], ins.at[3 + i]) for i, q in enumerate((q0, q1))]
    w_in.wait()
    for half in range(2):
        x_in[half].wait()
        project(bx.at[half], half, bw, "k", bk, place)
    wait_all(q_in)
    wait_all(write_logits([bq.at[0], bq.at[1]], bk, held, ls, sems))


def values_body(blocks, ready, place, *refs):
    n = 2 * blocks
    xs, made, wv, out = refs[:n], refs[n : n + sum(ready)], refs[n + sum(ready)], refs[n + sum(ready) + 1]
    bx, bw, held, ins, outs, moves = refs[n + sum(ready) + 2 :]
    rows = xs[0].shape[1]
    w_in = start(columns(wv, place), bw, ins.at[n])
    x_in = [start(x, bx.at[i], ins.at[i]) for i, x in enumerate(xs)]
    copies, made, block = [], list(made), 0
    for at, there in enumerate(ready):
        if there:
            copies.append(start(made.pop(0), out.at[:, pl.ds(at * rows, rows), :], moves.at[at]))
    w_in.wait()
    for at, there in enumerate(ready):
        if not there:
            for half in range(2):
                x_in[2 * block + half].wait()
                project(bx.at[2 * block + half], half, bw, "v", held.at[block], place)
            copies.append(
                start(held.at[block], out.at[:, pl.ds(at * rows, rows), :], outs.at[block])
            )
            block += 1
    wait_all(copies)


def make_values(place, blocks, made, ready, weight, name, late=()):
    seqs, rows, width = blocks[0][0].shape
    own = width // 2
    pairs, span = HEADS // 4, 2 * seqs * 2 * HEAD
    n = len(blocks)
    dma = pltpu.SemaphoreType.DMA
    return manual(
        functools.partial(values_body, n, ready),
        place,
        [*(a for b in blocks for a in b), *made, weight],
        [jax.ShapeDtypeStruct((pairs, rows * len(ready), span), BF16)],
        [
            pltpu.VMEM((2 * n, seqs, rows, width), BF16),
            pltpu.VMEM((width, own), BF16),
            pltpu.VMEM((n, pairs, rows, span), BF16),
            dma((2 * n + 1,)),
            dma((n,)),
            dma((len(ready),)),
        ],
        n * 4 * seqs * rows * width * own,
        name,
        late,
    )[0]


def add_body(count, place, *refs):
    out, parts = refs[-1], refs[:-1]
    z_lo = place[3]
    sums = []
    for n in range(0, len(parts), count):
        total = parts[n][...].astype(F32)
        for ref in parts[n + 1 : n + count]:
            total += ref[...].astype(F32)
        sums.append(total)
    total = jnp.concatenate(sums, axis=-1).astype(BF16)
    share = out.shape[2]
    for i in range(2):
        for z in range(PARTS):
            out[z, i ^ z_lo] = total[i, z * share : (z + 1) * share]


def add_parts(place, groups):
    parts = [a for g in groups for a in g]
    rows = parts[0].shape[1]
    cols = sum(g[0].shape[2] for g in groups)
    shape = (PARTS, 2, rows // PARTS, cols)
    return call(
        functools.partial(add_body, PARTS),
        place,
        parts,
        [whole(a.shape) for a in parts],
        [jax.ShapeDtypeStruct(shape, BF16)],
        [whole(shape)],
        (1,),
        sum(a.size for a in parts),
        "add_over_y",
    )[0]


def softmax_body(scale, place, parts, other, out, same):
    z_lo = place[3]
    sides = []
    for side in (z_lo, 1 - z_lo):
        total = parts[0, side].astype(F32)
        for z in range(1, PARTS):
            total += parts[z, side].astype(F32)
        sides.append(total)
    scaled = jnp.concatenate(sides, axis=-1) * scale
    expo = jnp.exp(scaled - jnp.max(scaled, axis=-1, keepdims=True))
    out[...] = (expo / jnp.sum(expo, axis=-1, keepdims=True)).astype(BF16)


def softmax(place, parts, scale, other):
    shape = (parts.shape[2], 2 * parts.shape[3])
    free = pl.BlockSpec(memory_space=pl.ANY)
    return pl.pallas_call(
        functools.partial(softmax_body, scale),
        out_shape=[
            jax.ShapeDtypeStruct(shape, BF16),
            jax.ShapeDtypeStruct(other.shape, other.dtype),
        ],
        in_specs=[pl.BlockSpec(memory_space=pltpu.SMEM), pl.BlockSpec(memory_space=pltpu.VMEM), free],
        out_specs=[pl.BlockSpec(memory_space=pltpu.VMEM), free],
        input_output_aliases={2: 1},
        compiler_params=pltpu.CompilerParams(vmem_limit_bytes=VMEM),
        cost_estimate=pl.CostEstimate(
            flops=parts.size * 8, bytes_accessed=parts.size * 4, transcendentals=parts.size // 4
        ),
        name="softmax",
    )(place, parts, other)


def order_body(place, *refs):
    out, parts = refs[-1], refs[:-1]
    for d, ref in enumerate(parts):
        out[rel(place[2] - d)] = ref[...]


def order(place, parts):
    shape = (PARTS, *parts[0].shape)
    return call(
        order_body,
        place,
        parts,
        [whole(a.shape) for a in parts],
        [jax.ShapeDtypeStruct(shape, BF16)],
        [whole(shape)],
        (1,),
        0,
        "order",
    )[0]


def mix_body(place, *refs):
    probs, values, outs = refs[:PARTS], refs[PARTS], refs[-2:]
    y = place[1]
    group = probs[0].shape[1] // 2
    lanes = 2 * HEAD
    seqs = outs[0].shape[0]
    p = jnp.concatenate([ref[0] for ref in probs], axis=0)
    got = jnp.dot(p, values[0], preferred_element_type=F32)
    first = lax.broadcasted_iota(jnp.int32, (group, lanes), 1) < HEAD
    for d in range(PARTS):
        at = pl.multiple_of(rel(y - d) * group, group)
        for s in range(2 * seqs):
            one, two = (
                got[(2 * d + h) * group : (2 * d + h + 1) * group, s * lanes : (s + 1) * lanes]
                for h in range(2)
            )
            outs[s // seqs][s % seqs, pl.ds(at, group), :] = jnp.where(first, one, two).astype(BF16)


def mix(place, probs, values, seqs):
    pairs, half, cols = probs[0].shape
    span = values.shape[2]
    rows = PARTS * half // 2
    lanes = 2 * HEAD
    shape = jax.ShapeDtypeStruct((seqs, rows, pairs * lanes), BF16)
    return call(
        mix_body,
        place,
        [*probs, values],
        [pl.BlockSpec((1, half, cols), lambda p, s: (p, 0, 0))] * PARTS
        + [pl.BlockSpec((1, cols, span), lambda p, s: (p, 0, 0))],
        [shape] * 2,
        [pl.BlockSpec((seqs, rows, lanes), lambda p, s: (0, 0, p))] * 2,
        (pairs,),
        2 * pairs * PARTS * half * cols * span,
        "mix",
    )


def finish_body(mine, theirs, weight_mine, weight_theirs, out):
    seqs, rows, own = mine.shape
    got = jnp.dot(mine[...].reshape(seqs * rows, own), weight_mine[...], preferred_element_type=F32)
    got += jnp.dot(
        theirs[...].reshape(seqs * rows, own), weight_theirs[...], preferred_element_type=F32
    )
    out[...] = got.astype(BF16).reshape(out.shape)


def finish(mine, theirs, weight_mine, weight_theirs):
    seqs, rows, own = mine.shape
    width = weight_mine.shape[1]
    part = seqs // 2
    return pl.pallas_call(
        finish_body,
        out_shape=jax.ShapeDtypeStruct((seqs, rows, width), BF16),
        grid=(seqs // part,),
        in_specs=[pl.BlockSpec((part, rows, own), lambda r: (r, 0, 0))] * 2
        + [pl.BlockSpec((own, width), lambda r: (0, 0))] * 2,
        out_specs=pl.BlockSpec((part, rows, width), lambda r: (r, 0, 0)),
        compiler_params=pltpu.CompilerParams(vmem_limit_bytes=VMEM),
        cost_estimate=pl.CostEstimate(
            flops=2 * seqs * rows * width * width,
            bytes_accessed=4 * seqs * rows * width + 2 * width * width,
            transcendentals=0,
        ),
        name="finish",
    )(mine, theirs, weight_mine, weight_theirs)


def ring_table(axis_of):
    return [
        (c * SIZE["x"] + i, c * SIZE["x"] + (i + (1 if c == axis_of else -1)) % SIZE["x"])
        for c in range(2)
        for i in range(SIZE["x"])
    ]


def send_x(arr, way):
    return lax.ppermute(arr, ("core", "x"), ring_table(way))


def per_device(data, query_matrix, key_matrix, value_matrix, output_matrix):
    seqs, rows, width = data.shape
    place = jnp.stack([lax.axis_index(a) for a in ("core", "y", "z_hi", "z_lo")])
    place = place.astype(jnp.int32)

    core = lax.axis_index("core")
    half = width // 2

    def swap(arr):
        return shift(arr, "core", 1)

    output_mine, output_theirs = (
        lax.dynamic_slice_in_dim(output_matrix, c * half, half, 0) for c in (core, 1 - core)
    )

    pairs, span, group = HEADS // 4, 4 * seqs * HEAD, rows // PARTS
    q_shape, k_shape = (pairs, PARTS, 2, group, span), (pairs, rows, span)
    dma = pltpu.SemaphoreType.DMA

    def logits_shape(n):
        return jax.ShapeDtypeStruct((2, pairs, 2 * group, n * rows), BF16)

    def bf(*shape):
        return pltpu.VMEM(shape, BF16)

    first, second = send_x(data, 0), send_x(data, 1)
    partner = shift(data, "z_lo", 1)
    queries, keys, values = manual(
        own_body,
        place,
        [data, swap(data), query_matrix, key_matrix, value_matrix],
        [jax.ShapeDtypeStruct(s, BF16) for s in (q_shape, k_shape, k_shape)],
        [bf(2, *data.shape), bf(3, width, half), bf(*q_shape), bf(*k_shape), bf(*k_shape)]
        + [dma((5,)), dma((3,))],
        12 * seqs * rows * width * half,
        "own",
    )
    first, second, partner = tie([first, second, partner], queries)
    far = send_x(first, 0)
    near = [(first, swap(second)), (second, swap(first))]
    partner2 = (partner, swap(partner))
    partner_queries, *near_logits = manual(
        near_body,
        place,
        [queries, keys, *partner2, *near[0], *near[1], query_matrix, key_matrix],
        [jax.ShapeDtypeStruct(q_shape, BF16)] + [logits_shape(3)] * PARTS,
        [bf(6, *data.shape), bf(2, width, half), bf(2, *q_shape), bf(pairs, 3 * rows, span)]
        + [bf(PARTS, 2, pairs, 2 * group, 3 * rows), dma((10,)), dma((1,)), dma((pairs, PARTS))],
        12 * seqs * rows * width * half,
        "near",
    )
    (far,) = tie([far], partner_queries)
    far2 = (far, swap(far))
    far_logits = manual(
        far_body,
        place,
        [queries, partner_queries, *far2, key_matrix],
        [logits_shape(1)] * PARTS,
        [bf(2, *data.shape), bf(width, half), bf(2, *q_shape), bf(*k_shape)]
        + [bf(PARTS, 2, pairs, 2 * group, rows), dma((5,)), dma((pairs, PARTS))],
        4 * seqs * rows * width * half,
        "far",
    )

    def over_y(parts):
        parts = [a.reshape(2, -1, a.shape[-1]) for a in parts]
        return [parts[0]] + [shift(parts[d], "y", d) for d in range(1, PARTS)]

    groups = [over_y(near_logits), over_y(far_logits)]
    z_own = make_values(
        place, [partner2], [], [False], value_matrix, "values_partner", far_logits[:1]
    )
    z_first, z_second = send_x(z_own, 0), send_x(z_own, 1)
    sent = add_parts(place, groups)

    sent = sent.reshape(2 * PARTS, *sent.shape[2:])
    got = lax.all_to_all(sent, ("z_hi", "z_lo"), 0, 0, tiled=True)
    got = got.reshape(PARTS, 2, *got.shape[1:])
    all_rows = seqs * lax.axis_size(("z_hi", "y", "core"))
    probs, z_first = softmax(place, got, HEAD ** (-0.5) * all_rows ** (-0.5), z_first)
    z_far = send_x(z_first, 0)
    probs = order(place, [probs] + [shift(probs, "z_hi", d) for d in range(1, PARTS)])
    probs = probs.reshape(pairs, 2 * group, probs.shape[-1])
    values = make_values(
        place,
        [*near, far2],
        [values, z_own, z_first, z_second, z_far],
        [True, False, False, False, True, True, True, True],
        value_matrix,
        "values",
    )
    probs = [probs] + [shift(probs, "y", d) for d in range(1, PARTS)]
    mine, theirs = mix(place, probs, values, seqs)
    return finish(mine, swap(theirs), output_mine, output_theirs)


def solution(mesh):
    fine = Mesh(mesh.devices.reshape(SIZES), AXES)
    spec = P(("z_hi", "y", "core"), ("x", "z_lo"), None)
    return jax.shard_map(
        per_device,
        mesh=fine,
        in_specs=(spec, P(), P(), P(), P()),
        out_specs=spec,
        check_vma=False,
    )
```

```python
import functools

import jax
import jax.numpy as jnp
from jax import lax
from jax.experimental import pallas as pl
from jax.experimental.pallas import tpu as pltpu
from jax.sharding import Mesh, PartitionSpec as P

HEADS = 12
HEAD = 64
AXES = ("z_hi", "y", "core", "x", "z_lo")
SIZES = (4, 4, 2, 4, 2)
SIZE = dict(zip(AXES, SIZES))
BF16 = jnp.bfloat16
F32 = jnp.float32
PARTS = 4
VMEM = 16 << 20


def shift(arr, axis, step):
    n = SIZE[axis]
    return lax.ppermute(arr, axis, [(i, (i + step) % n) for i in range(n)])


def whole(shape):
    return pl.BlockSpec(shape, lambda *_: (0,) * len(shape), pipeline_mode=pl.Buffered(1))


def call(body, place, ins, in_specs, outs, out_specs, grid, flops, name, late=()):
    moved = sum(a.size * a.dtype.itemsize for a in ins)
    moved += sum(o.size * o.dtype.itemsize for o in outs)
    n = 1 + len(ins)

    def run(*refs):
        body(*refs[:n], *refs[n + len(late) :])

    in_specs = [*in_specs] + [pl.BlockSpec(memory_space=pl.ANY)] * len(late)
    return pl.pallas_call(
        run,
        out_shape=outs,
        grid_spec=pltpu.PrefetchScalarGridSpec(
            num_scalar_prefetch=1, grid=grid, in_specs=in_specs, out_specs=out_specs
        ),
        compiler_params=pltpu.CompilerParams(vmem_limit_bytes=VMEM),
        cost_estimate=pl.CostEstimate(flops=flops, bytes_accessed=moved, transcendentals=0),
        name=name,
    )(place, *ins, *late)


def tie(arrays, late):
    n = len(arrays)
    free = pl.BlockSpec(memory_space=pl.ANY)
    return pl.pallas_call(
        lambda *refs: None,
        out_shape=[jax.ShapeDtypeStruct(a.shape, a.dtype) for a in arrays],
        in_specs=[free] * (n + 1),
        out_specs=[free] * n,
        input_output_aliases={i: i for i in range(n)},
        compiler_params=pltpu.CompilerParams(vmem_limit_bytes=1 << 20),
        name="tie",
    )(*arrays, late)


def rel(index):
    return lax.rem(index + PARTS, PARTS)


def manual(body, place, ins, outs, scratch, flops, name, late=()):
    moved = sum(a.size * a.dtype.itemsize for a in ins)
    moved += sum(o.size * o.dtype.itemsize for o in outs)
    n = 1 + len(ins)
    far_off = pl.BlockSpec(memory_space=pltpu.HBM)

    def run(*refs):
        body(*refs[:n], *refs[n + len(late) :])

    return pl.pallas_call(
        run,
        out_shape=outs,
        in_specs=[pl.BlockSpec(memory_space=pltpu.SMEM)]
        + [far_off] * len(ins)
        + [pl.BlockSpec(memory_space=pl.ANY)] * len(late),
        out_specs=[far_off] * len(outs),
        scratch_shapes=scratch,
        compiler_params=pltpu.CompilerParams(vmem_limit_bytes=VMEM),
        cost_estimate=pl.CostEstimate(flops=flops, bytes_accessed=moved, transcendentals=0),
        name=name,
    )(place, *ins, *late)


def local(body, place, ins, outs, flops, name, late=()):
    here = pl.BlockSpec(memory_space=pltpu.VMEM)
    moved = sum(a.size * a.dtype.itemsize for a in ins)
    moved += sum(o.size * o.dtype.itemsize for o in outs)
    n = 1 + len(ins)

    def run(*refs):
        body(*refs[:n], *refs[n + len(late) :])

    return pl.pallas_call(
        run,
        out_shape=outs,
        in_specs=[pl.BlockSpec(memory_space=pltpu.SMEM)] + [here] * len(ins)
        + [pl.BlockSpec(memory_space=pl.ANY)] * len(late),
        out_specs=[here] * len(outs),
        compiler_params=pltpu.CompilerParams(vmem_limit_bytes=VMEM),
        cost_estimate=pl.CostEstimate(flops=flops, bytes_accessed=moved, transcendentals=0),
        name=name,
    )(place, *ins, *late)


def start(src, dst, sem):
    copy = pltpu.make_async_copy(src, dst, sem)
    copy.start()
    return copy


def columns(weight, place):
    own = weight.shape[1] // 2
    return weight.at[:, pl.ds(pl.multiple_of(place[0] * own, own), own)]


def project(x_ref, half, weight, kind, out, place, base=0):
    seqs, rows, width = x_ref.shape
    lanes = 2 * HEAD
    pairs = weight.shape[1] // lanes
    group = rows // PARTS
    x = x_ref[...].reshape(seqs * rows, width)
    got = jnp.dot(x, weight[...], preferred_element_type=F32).astype(BF16)
    for s in range(seqs):
        at = (half * seqs + s) * lanes
        for p in range(pairs):
            part = got[s * rows : (s + 1) * rows, p * lanes : (p + 1) * lanes]
            if kind != "q":
                out[p, base : base + rows, at : at + lanes] = part
                continue
            first = lax.broadcasted_iota(jnp.int32, part.shape, 1) < HEAD
            for h in range(2):
                kept = jnp.where(first == (h == 0), part, jnp.zeros_like(part))
                for a in range(PARTS):
                    out[p, rel(a - place[1]), h, :, at : at + lanes] = kept[
                        a * group : (a + 1) * group
                    ]


def write_logits(queries, keys, outs):
    half = outs[0].shape[2]
    for p in range(outs[0].shape[1]):
        k = jnp.concatenate([ref[p] for ref in keys], axis=0)
        for i, refs in enumerate(queries):
            q = jnp.concatenate([ref[p].reshape(PARTS * half, -1) for ref in refs], axis=-1)
            got = lax.dot_general(q, k, (((1,), (1,)), ((), ())), preferred_element_type=F32)
            for d, out in enumerate(outs):
                out[i, p] = got[d * half : (d + 1) * half].astype(BF16)


def wait_all(copies):
    for copy in copies:
        copy.wait()


def own_body(place, x0, x1, wq, wk, wv, oq, ok, ov, bx, bw, bq, bk, bv, ins, outs):
    loads = [start(x, bx.at[i], ins.at[i]) for i, x in enumerate((x0, x1))]
    loads += [start(columns(w, place), bw.at[i], ins.at[2 + i]) for i, w in enumerate((wq, wk, wv))]
    stores = []
    for i, (kind, out, held) in enumerate((("q", oq, bq), ("k", ok, bk), ("v", ov, bv))):
        loads[2 + i].wait()
        for half in range(2):
            if i == 0:
                loads[half].wait()
            project(bx.at[half], half, bw.at[i], kind, held, place)
        stores.append(start(held, out, outs.at[i]))
    wait_all(stores)


def near_body(place, first, second, partner, wq, wk, qa, k1, k2):
    project(first, 0, columns(wk, place), "k", k1, place)
    project(second, 0, columns(wk, place), "k", k2, place)
    project(partner, 0, columns(wq, place), "q", qa, place)


def near_keys_body(place, a1, a2, first, second, wk, k1, k2):
    half = a1.shape[2]
    for a, x, k in ((a1, first, k1), (a2, second, k2)):
        k[:, :, :half] = a[...]
        project(x, 1, columns(wk, place), "k", k, place)


def near_logits_body(place, q0, qa, k0, k1, k2, partner, wq, qb, *outs):
    project(partner, 0, columns(wq, place), "q", qb, place)
    write_logits([[q0], [qa, qb]], [k0, k1, k2], outs)


def far_logits_body(place, q0, qa, qb, k, *outs):
    write_logits([[q0], [qa, qb]], [k], outs)


def values_body(place, *refs):
    *xs, weight = refs[: len(refs) * 2 // 3 + 1]
    for i, out in enumerate(refs[len(xs) + 1 :]):
        for half in range(2):
            project(xs[2 * i + half], half, columns(weight, place), "v", out, place)


def gather_body(place, *refs):
    out, at = refs[-1], 0
    for ref in refs[:-1]:
        rows = ref.shape[1]
        out[:, at : at + rows, :] = ref[...]
        at += rows


def add_body(count, place, *refs):
    out, parts = refs[-1], refs[:-1]
    z_lo = place[3]
    sums = []
    for n in range(0, len(parts), count):
        total = parts[n][...].astype(F32)
        for ref in parts[n + 1 : n + count]:
            total += ref[...].astype(F32)
        sums.append(total)
    total = jnp.concatenate(sums, axis=-1).astype(BF16)
    share = out.shape[2]
    for i in range(2):
        for z in range(PARTS):
            out[z, i ^ z_lo] = total[i, z * share : (z + 1) * share]


def add_parts(place, groups):
    parts = [a for g in groups for a in g]
    rows = parts[0].shape[1]
    cols = sum(g[0].shape[2] for g in groups)
    return local(
        functools.partial(add_body, PARTS),
        place,
        parts,
        [jax.ShapeDtypeStruct((PARTS, 2, rows // PARTS, cols), BF16)],
        sum(a.size for a in parts),
        "add_over_y",
    )[0]


def softmax_body(scale, place, parts, *refs):
    out = refs[len(refs) // 2]
    z_lo = place[3]
    sides = []
    for side in (z_lo, 1 - z_lo):
        total = parts[0, side].astype(F32)
        for z in range(1, PARTS):
            total += parts[z, side].astype(F32)
        sides.append(total)
    scaled = jnp.concatenate(sides, axis=-1) * scale
    expo = jnp.exp(scaled - jnp.max(scaled, axis=-1, keepdims=True))
    out[...] = (expo / jnp.sum(expo, axis=-1, keepdims=True)).astype(BF16)


def softmax(place, parts, scale, others):
    shape = (parts.shape[2], 2 * parts.shape[3])
    free = [pl.BlockSpec(memory_space=pl.ANY)] * len(others)
    here = pl.BlockSpec(memory_space=pltpu.VMEM)
    return pl.pallas_call(
        functools.partial(softmax_body, scale),
        out_shape=[jax.ShapeDtypeStruct(shape, BF16)]
        + [jax.ShapeDtypeStruct(a.shape, a.dtype) for a in others],
        in_specs=[pl.BlockSpec(memory_space=pltpu.SMEM), here, *free],
        out_specs=[here, *free],
        input_output_aliases={2 + i: 1 + i for i in range(len(others))},
        compiler_params=pltpu.CompilerParams(vmem_limit_bytes=VMEM),
        cost_estimate=pl.CostEstimate(
            flops=parts.size * 8, bytes_accessed=parts.size * 4, transcendentals=parts.size // 4
        ),
        name="softmax",
    )(place, parts, *others)


def order_body(place, *refs):
    out, parts = refs[-1], refs[:-1]
    for d, ref in enumerate(parts):
        out[rel(place[2] - d)] = ref[...]


def order(place, parts):
    shape = (PARTS, *parts[0].shape)
    return call(
        order_body,
        place,
        parts,
        [whole(a.shape) for a in parts],
        [jax.ShapeDtypeStruct(shape, BF16)],
        [whole(shape)],
        (1,),
        0,
        "order",
    )[0]


def mix_body(place, *refs):
    probs, values, outs = refs[:PARTS], refs[PARTS], refs[-2:]
    y = place[1]
    pairs, half, _ = probs[0].shape
    group = half // 2
    lanes = 2 * HEAD
    seqs = outs[0].shape[0]
    first = lax.broadcasted_iota(jnp.int32, (group, lanes), 1) < HEAD
    for pair in range(pairs):
        p = jnp.concatenate([ref[pair] for ref in probs], axis=0)
        got = jnp.dot(p, values[pair], preferred_element_type=F32)
        for d in range(PARTS):
            at = pl.multiple_of(rel(y - d) * group, group)
            for s in range(2 * seqs):
                one, two = (
                    got[(2 * d + h) * group : (2 * d + h + 1) * group, s * lanes : (s + 1) * lanes]
                    for h in range(2)
                )
                outs[s // seqs][
                    s % seqs, pl.ds(at, group), pair * lanes : (pair + 1) * lanes
                ] = jnp.where(first, one, two).astype(BF16)


def mix(place, probs, values, seqs):
    pairs, half, cols = probs[0].shape
    rows = PARTS * half // 2
    return local(
        mix_body,
        place,
        [*probs, values],
        [jax.ShapeDtypeStruct((seqs, rows, pairs * 2 * HEAD), BF16)] * 2,
        2 * pairs * PARTS * half * cols * values.shape[2],
        "mix",
    )


def finish_body(mine, theirs, weight_mine, weight_theirs, out):
    seqs, rows, own = mine.shape
    got = jnp.dot(mine[...].reshape(seqs * rows, own), weight_mine[...], preferred_element_type=F32)
    got += jnp.dot(
        theirs[...].reshape(seqs * rows, own), weight_theirs[...], preferred_element_type=F32
    )
    out[...] = got.astype(BF16).reshape(out.shape)


def finish(mine, theirs, weight_mine, weight_theirs):
    seqs, rows, own = mine.shape
    width = weight_mine.shape[1]
    part = seqs // 2
    return pl.pallas_call(
        finish_body,
        out_shape=jax.ShapeDtypeStruct((seqs, rows, width), BF16),
        grid=(seqs // part,),
        in_specs=[pl.BlockSpec((part, rows, own), lambda r: (r, 0, 0))] * 2
        + [pl.BlockSpec((own, width), lambda r: (0, 0))] * 2,
        out_specs=pl.BlockSpec((part, rows, width), lambda r: (r, 0, 0)),
        compiler_params=pltpu.CompilerParams(vmem_limit_bytes=VMEM),
        cost_estimate=pl.CostEstimate(
            flops=2 * seqs * rows * width * width,
            bytes_accessed=4 * seqs * rows * width + 2 * width * width,
            transcendentals=0,
        ),
        name="finish",
    )(mine, theirs, weight_mine, weight_theirs)


def ring_table(axis_of):
    return [
        (c * SIZE["x"] + i, c * SIZE["x"] + (i + (1 if c == axis_of else -1)) % SIZE["x"])
        for c in range(2)
        for i in range(SIZE["x"])
    ]


def send_x(arr, way):
    return lax.ppermute(arr, ("core", "x"), ring_table(way))


def per_device(data, query_matrix, key_matrix, value_matrix, output_matrix):
    seqs, rows, width = data.shape
    place = jnp.stack([lax.axis_index(a) for a in ("core", "y", "z_hi", "z_lo")])
    place = place.astype(jnp.int32)

    core = lax.axis_index("core")
    half = width // 2

    def swap(arr):
        return shift(arr, "core", 1)

    output_mine, output_theirs = (
        lax.dynamic_slice_in_dim(output_matrix, c * half, half, 0) for c in (core, 1 - core)
    )

    pairs, span, group = HEADS // 4, 4 * seqs * HEAD, rows // PARTS
    q_shape, k_shape = (pairs, PARTS, 2, group, span), (pairs, rows, span)
    dma = pltpu.SemaphoreType.DMA

    def logits_shape(n):
        return jax.ShapeDtypeStruct((2, pairs, 2 * group, n * rows), BF16)

    def bf(*shape):
        return pltpu.VMEM(shape, BF16)

    first, second = send_x(data, 0), send_x(data, 1)
    partner = shift(data, "z_lo", 1)
    queries, keys, values = manual(
        own_body,
        place,
        [data, swap(data), query_matrix, key_matrix, value_matrix],
        [jax.ShapeDtypeStruct(s, BF16) for s in (q_shape, k_shape, k_shape)],
        [bf(2, *data.shape), bf(3, width, half), bf(*q_shape), bf(*k_shape), bf(*k_shape)]
        + [dma((5,)), dma((3,))],
        12 * seqs * rows * width * half,
        "own",
    )
    first, second, partner = (tie([a], queries)[0] for a in (first, second, partner))
    near = [(first, swap(second)), (second, swap(first))]
    partner2 = (partner, swap(partner))
    qa_shape, ka_shape = (*q_shape[:-1], span // 2), (*k_shape[:-1], span // 2)

    def of(*shapes):
        return [jax.ShapeDtypeStruct(s, BF16) for s in shapes]

    work = 4 * seqs * rows * width * half
    qa, ka1, ka2 = local(
        near_body,
        place,
        [first, second, partner, query_matrix, key_matrix],
        of(qa_shape, ka_shape, ka_shape),
        3 * work // 2,
        "near",
    )
    k1, k2 = local(
        near_keys_body,
        place,
        [ka1, ka2, near[0][1], near[1][1], key_matrix],
        of(k_shape, k_shape),
        work,
        "near_keys",
    )
    far_keys = send_x(k1, 0)
    qb, *near_logits = local(
        near_logits_body,
        place,
        [queries, qa, keys, k1, k2, partner2[1], query_matrix],
        of(qa_shape) + [logits_shape(3)] * PARTS,
        2 * work,
        "near_logits",
    )
    (z_own,) = local(
        values_body,
        place,
        [*partner2, value_matrix],
        of(k_shape),
        work,
        "values_partner",
        [qb],
    )
    z_first, z_second = send_x(z_own, 0), send_x(z_own, 1)
    far_logits = local(
        far_logits_body,
        place,
        [queries, qa, qb, far_keys],
        [logits_shape(1)] * PARTS,
        work // 2,
        "far_logits",
        [z_own],
    )
    def over_y(parts):
        parts = [a.reshape(2, -1, a.shape[-1]) for a in parts]
        return [parts[0]] + [shift(parts[d], "y", d) for d in range(1, PARTS)]

    groups = [over_y(near_logits), over_y(far_logits)]
    sent = add_parts(place, groups)
    first_values, second_values = local(
        values_body,
        place,
        [*near[0], *near[1], value_matrix],
        of(k_shape, k_shape),
        2 * work,
        "values_near",
        [far_logits[0]],
    )

    sent = sent.reshape(2 * PARTS, *sent.shape[2:])
    got = lax.all_to_all(sent, ("z_hi", "z_lo"), 0, 0, tiled=True)
    got = got.reshape(PARTS, 2, *got.shape[1:])
    all_rows = seqs * lax.axis_size(("z_hi", "y", "core"))
    scale = HEAD ** (-0.5) * all_rows ** (-0.5)
    probs, z_first, z_second, first_values = softmax(
        place, got, scale, [z_first, z_second, first_values]
    )
    z_far = send_x(z_first, 0)
    far_values = send_x(first_values, 0)
    probs = order(place, [probs] + [shift(probs, "z_hi", d) for d in range(1, PARTS)])
    probs = probs.reshape(pairs, 2 * group, probs.shape[-1])
    parts = [values, first_values, second_values, far_values, z_own, z_first, z_second, z_far]
    (values,) = local(gather_body, place, parts, of((pairs, 8 * rows, span)), 0, "gather_values")
    probs = [probs] + [shift(probs, "y", d) for d in range(1, PARTS)]
    mine, theirs = mix(place, probs, values, seqs)
    return finish(mine, swap(theirs), output_mine, output_theirs)


def solution(mesh):
    fine = Mesh(mesh.devices.reshape(SIZES), AXES)
    spec = P(("z_hi", "y", "core"), ("x", "z_lo"), None)
    return jax.shard_map(
        per_device,
        mesh=fine,
        in_specs=(spec, P(), P(), P(), P()),
        out_specs=spec,
        check_vma=False,
    )
```

```python
import functools

import jax
import jax.numpy as jnp
from jax import lax
from jax.experimental import pallas as pl
from jax.experimental.pallas import tpu as pltpu
from jax.sharding import Mesh, PartitionSpec as P

HEADS = 12
HEAD = 64
AXES = ("z_hi", "y", "core", "x", "z_lo")
SIZES = (4, 4, 2, 4, 2)
SIZE = dict(zip(AXES, SIZES))
BF16 = jnp.bfloat16
F32 = jnp.float32
PARTS = 4
VMEM = 16 << 20


def shift(arr, axis, step):
    n = SIZE[axis]
    return lax.ppermute(arr, axis, [(i, (i + step) % n) for i in range(n)])


def whole(shape):
    return pl.BlockSpec(shape, lambda *_: (0,) * len(shape), pipeline_mode=pl.Buffered(1))


def call(body, place, ins, in_specs, outs, out_specs, grid, flops, name, late=()):
    moved = sum(a.size * a.dtype.itemsize for a in ins)
    moved += sum(o.size * o.dtype.itemsize for o in outs)
    n = 1 + len(ins)

    def run(*refs):
        body(*refs[:n], *refs[n + len(late) :])

    in_specs = [*in_specs] + [pl.BlockSpec(memory_space=pl.ANY)] * len(late)
    return pl.pallas_call(
        run,
        out_shape=outs,
        grid_spec=pltpu.PrefetchScalarGridSpec(
            num_scalar_prefetch=1, grid=grid, in_specs=in_specs, out_specs=out_specs
        ),
        compiler_params=pltpu.CompilerParams(vmem_limit_bytes=VMEM),
        cost_estimate=pl.CostEstimate(flops=flops, bytes_accessed=moved, transcendentals=0),
        name=name,
    )(place, *ins, *late)


def tie(arrays, late):
    n = len(arrays)
    free = pl.BlockSpec(memory_space=pl.ANY)
    return pl.pallas_call(
        lambda *refs: None,
        out_shape=[jax.ShapeDtypeStruct(a.shape, a.dtype) for a in arrays],
        in_specs=[free] * (n + 1),
        out_specs=[free] * n,
        input_output_aliases={i: i for i in range(n)},
        compiler_params=pltpu.CompilerParams(vmem_limit_bytes=1 << 20),
        name="tie",
    )(*arrays, late)


def rel(index):
    return lax.rem(index + PARTS, PARTS)


def manual(body, place, ins, outs, scratch, flops, name, late=()):
    moved = sum(a.size * a.dtype.itemsize for a in ins)
    moved += sum(o.size * o.dtype.itemsize for o in outs)
    n = 1 + len(ins)
    far_off = pl.BlockSpec(memory_space=pltpu.HBM)

    def run(*refs):
        body(*refs[:n], *refs[n + len(late) :])

    return pl.pallas_call(
        run,
        out_shape=outs,
        in_specs=[pl.BlockSpec(memory_space=pltpu.SMEM)]
        + [far_off] * len(ins)
        + [pl.BlockSpec(memory_space=pl.ANY)] * len(late),
        out_specs=[far_off] * len(outs),
        scratch_shapes=scratch,
        compiler_params=pltpu.CompilerParams(vmem_limit_bytes=VMEM),
        cost_estimate=pl.CostEstimate(flops=flops, bytes_accessed=moved, transcendentals=0),
        name=name,
    )(place, *ins, *late)


def local(body, place, ins, outs, flops, name, late=()):
    here = pl.BlockSpec(memory_space=pltpu.VMEM)
    moved = sum(a.size * a.dtype.itemsize for a in ins)
    moved += sum(o.size * o.dtype.itemsize for o in outs)
    n = 1 + len(ins)

    def run(*refs):
        body(*refs[:n], *refs[n + len(late) :])

    return pl.pallas_call(
        run,
        out_shape=outs,
        in_specs=[pl.BlockSpec(memory_space=pltpu.SMEM)] + [here] * len(ins)
        + [pl.BlockSpec(memory_space=pl.ANY)] * len(late),
        out_specs=[here] * len(outs),
        compiler_params=pltpu.CompilerParams(vmem_limit_bytes=VMEM),
        cost_estimate=pl.CostEstimate(flops=flops, bytes_accessed=moved, transcendentals=0),
        name=name,
    )(place, *ins, *late)


def start(src, dst, sem):
    copy = pltpu.make_async_copy(src, dst, sem)
    copy.start()
    return copy


def columns(weight, place):
    own = weight.shape[1] // 2
    return weight.at[:, pl.ds(pl.multiple_of(place[0] * own, own), own)]


def project(x_ref, half, weight, out, place):
    seqs, rows, width = x_ref.shape
    lanes = 2 * HEAD
    got = jnp.dot(
        x_ref[...].reshape(seqs * rows, width), weight[...], preferred_element_type=F32
    ).astype(BF16)
    for s in range(seqs):
        at = (half * seqs + s) * lanes
        for p in range(out.shape[0]):
            out[p, :, at : at + lanes] = got[s * rows : (s + 1) * rows, p * lanes : (p + 1) * lanes]


def project_heads(x_ref, half, weights, out, place):
    seqs, rows, width = x_ref.shape
    lanes, some = 2 * HEAD, seqs // 2
    group = rows // PARTS
    sides = [
        jnp.dot(
            x_ref[i * some : (i + 1) * some].reshape(some * rows, width),
            weights[i],
            preferred_element_type=F32,
        ).astype(BF16)
        for i in range(2)
    ]
    first = lax.broadcasted_iota(jnp.int32, (rows, lanes), 1) < HEAD
    for s in range(some):
        at = (half * some + s) * lanes
        for p in range(out.shape[0] // 2):
            one, two = (a[s * rows : (s + 1) * rows, p * lanes : (p + 1) * lanes] for a in sides)
            for h in range(2):
                part = jnp.where(first, two, one) if h else jnp.where(first, one, two)
                if len(out.shape) == 3:
                    out[2 * p + h, :, at : at + lanes] = part
                    continue
                for a in range(PARTS):
                    out[2 * p + h, rel(a - place[1]), :, at : at + lanes] = part[
                        a * group : (a + 1) * group
                    ]


def write_logits(queries, keys, outs):
    group = outs[0].shape[2] // 2
    for head in range(keys[0].shape[0]):
        k = jnp.concatenate([ref[head] for ref in keys], axis=0)
        q = jnp.concatenate(
            [
                jnp.concatenate([ref[head].reshape(PARTS * group, -1) for ref in refs], axis=-1)
                for refs in queries
            ],
            axis=0,
        )
        got = lax.dot_general(q, k, (((1,), (1,)), ((), ())), preferred_element_type=F32)
        at = head % 2 * group
        for i in range(len(queries)):
            for d, out in enumerate(outs):
                out[i, head // 2, at : at + group] = got[
                    (i * PARTS + d) * group : (i * PARTS + d + 1) * group
                ].astype(BF16)


def wait_all(copies):
    for copy in copies:
        copy.wait()


def own_body(place, x0, x1, wq, wk, wv, oq, ok, ov, oqw, okw, bx, bw, bq, bk, bv, bs, ins, outs):
    loads = [start(x, bx.at[i], ins.at[i]) for i, x in enumerate((x0, x1))]
    loads += [start(columns(w, place), bw.at[i], ins.at[2 + i]) for i, w in enumerate((wq, wk, wv))]
    lanes = 2 * HEAD
    stores = []
    for i, out in enumerate((oqw, okw)):
        loads[2 + i].wait()
        bs[i, 0] = bw[i]
        for p in range(bw.shape[2] // lanes):
            at = slice(p * lanes, (p + 1) * lanes)
            bs[i, 1, :, at] = pltpu.roll(bw[i, :, at].astype(F32), HEAD, 1).astype(BF16)
        stores.append(start(bs.at[i], out, outs.at[3 + i]))
    for load in loads[:2]:
        load.wait()
    for i, (out, held) in enumerate(((oq, bq), (ok, bk))):
        for half in range(2):
            project_heads(bx.at[half], half, bs.at[i], held, place)
        stores.append(start(held, out, outs.at[i]))
    loads[4].wait()
    for half in range(2):
        project(bx.at[half], half, bw.at[2], bv, place)
    stores.append(start(bv, ov, outs.at[2]))
    wait_all(stores)


def near_body(place, first, second, partner, wq, wk, qa, k1, k2):
    project_heads(first, 0, wk, k1, place)
    project_heads(second, 0, wk, k2, place)
    project_heads(partner, 0, wq, qa, place)


def near_keys_body(place, a1, a2, first, second, wk, k1, k2):
    half = a1.shape[2]
    for a, x, k in ((a1, first, k1), (a2, second, k2)):
        k[:, :, :half] = a[...]
        project_heads(x, 1, wk, k, place)


def near_logits_body(place, q0, qa, k0, k1, k2, partner, wq, qb, *outs):
    project_heads(partner, 0, wq, qb, place)
    write_logits([[q0], [qa, qb]], [k0, k1, k2], outs)


def far_logits_body(place, q0, qa, qb, k, *outs):
    write_logits([[q0], [qa, qb]], [k], outs)


def values_body(place, *refs):
    *xs, weight = refs[: len(refs) * 2 // 3 + 1]
    for i, out in enumerate(refs[len(xs) + 1 :]):
        for half in range(2):
            project(xs[2 * i + half], half, columns(weight, place), out, place)


def near_values_body(place, x0, x1, x2, x3, z_first, weight, both, second):
    for half, x in enumerate((x0, x1)):
        project(x, half, columns(weight, place), both.at[0], place)
    for half, x in enumerate((x2, x3)):
        project(x, half, columns(weight, place), second, place)
    both[1] = z_first[...]


def gather_body(place, own, both, second, far, z_own, z_second, out):
    blocks = (own, both.at[0], second, far.at[0], z_own, both.at[1], z_second, far.at[1])
    rows = own.shape[1]
    for i, ref in enumerate(blocks):
        out[:, i * rows : (i + 1) * rows, :] = ref[...]


def add_body(count, place, *refs):
    out, parts = refs[-1], refs[:-1]
    z_lo = place[3]
    sums = []
    for n in range(0, len(parts), count):
        total = parts[n][...].astype(F32)
        for ref in parts[n + 1 : n + count]:
            total += ref[...].astype(F32)
        sums.append(total)
    total = jnp.concatenate(sums, axis=-1).astype(BF16)
    share = out.shape[2]
    for i in range(2):
        for z in range(PARTS):
            out[z, i ^ z_lo] = total[i, z * share : (z + 1) * share]


def add_parts(place, groups):
    parts = [a for g in groups for a in g]
    rows = parts[0].shape[1]
    cols = sum(g[0].shape[2] for g in groups)
    return local(
        functools.partial(add_body, PARTS),
        place,
        parts,
        [jax.ShapeDtypeStruct((PARTS, 2, rows // PARTS, cols), BF16)],
        sum(a.size for a in parts),
        "add_over_y",
    )[0]


def softmax_body(scale, place, parts, *refs):
    out = refs[len(refs) // 2]
    z_lo = place[3]
    sides = []
    for side in (z_lo, 1 - z_lo):
        total = parts[0, side].astype(F32)
        for z in range(1, PARTS):
            total += parts[z, side].astype(F32)
        sides.append(total)
    scaled = jnp.concatenate(sides, axis=-1) * scale
    expo = jnp.exp(scaled - jnp.max(scaled, axis=-1, keepdims=True))
    out[...] = (expo / jnp.sum(expo, axis=-1, keepdims=True)).astype(BF16)


def softmax(place, parts, scale, others):
    shape = (parts.shape[2], 2 * parts.shape[3])
    free = [pl.BlockSpec(memory_space=pl.ANY)] * len(others)
    here = pl.BlockSpec(memory_space=pltpu.VMEM)
    return pl.pallas_call(
        functools.partial(softmax_body, scale),
        out_shape=[jax.ShapeDtypeStruct(shape, BF16)]
        + [jax.ShapeDtypeStruct(a.shape, a.dtype) for a in others],
        in_specs=[pl.BlockSpec(memory_space=pltpu.SMEM), here, *free],
        out_specs=[here, *free],
        input_output_aliases={2 + i: 1 + i for i in range(len(others))},
        compiler_params=pltpu.CompilerParams(vmem_limit_bytes=VMEM),
        cost_estimate=pl.CostEstimate(
            flops=parts.size * 8, bytes_accessed=parts.size * 4, transcendentals=parts.size // 4
        ),
        name="softmax",
    )(place, parts, *others)


def order_body(place, *refs):
    out, parts = refs[-1], refs[:-1]
    for d, ref in enumerate(parts):
        out[rel(place[2] - d)] = ref[...]


def order(place, parts):
    shape = (PARTS, *parts[0].shape)
    return call(
        order_body,
        place,
        parts,
        [whole(a.shape) for a in parts],
        [jax.ShapeDtypeStruct(shape, BF16)],
        [whole(shape)],
        (1,),
        0,
        "order",
    )[0]


def mix_body(place, *refs):
    probs, values, outs = refs[:PARTS], refs[PARTS], refs[-2:]
    y = place[1]
    pairs, half, _ = probs[0].shape
    group = half // 2
    lanes = 2 * HEAD
    seqs = outs[0].shape[0]
    first = lax.broadcasted_iota(jnp.int32, (group, lanes), 1) < HEAD
    for pair in range(pairs):
        p = jnp.concatenate([ref[pair] for ref in probs], axis=0)
        got = jnp.dot(p, values[pair], preferred_element_type=F32)
        for d in range(PARTS):
            at = pl.multiple_of(rel(y - d) * group, group)
            for s in range(2 * seqs):
                one, two = (
                    got[(2 * d + h) * group : (2 * d + h + 1) * group, s * lanes : (s + 1) * lanes]
                    for h in range(2)
                )
                outs[s // seqs][
                    s % seqs, pl.ds(at, group), pair * lanes : (pair + 1) * lanes
                ] = jnp.where(first, one, two).astype(BF16)


def mix(place, probs, values, seqs):
    pairs, half, cols = probs[0].shape
    rows = PARTS * half // 2
    return local(
        mix_body,
        place,
        [*probs, values],
        [jax.ShapeDtypeStruct((seqs, rows, pairs * 2 * HEAD), BF16)] * 2,
        2 * pairs * PARTS * half * cols * values.shape[2],
        "mix",
    )


def finish_body(mine, theirs, weight_mine, weight_theirs, out):
    seqs, rows, own = mine.shape
    got = jnp.dot(mine[...].reshape(seqs * rows, own), weight_mine[...], preferred_element_type=F32)
    got += jnp.dot(
        theirs[...].reshape(seqs * rows, own), weight_theirs[...], preferred_element_type=F32
    )
    out[...] = got.astype(BF16).reshape(out.shape)


def finish(mine, theirs, weight_mine, weight_theirs):
    seqs, rows, own = mine.shape
    width = weight_mine.shape[1]
    part = seqs // 2
    return pl.pallas_call(
        finish_body,
        out_shape=jax.ShapeDtypeStruct((seqs, rows, width), BF16),
        grid=(seqs // part,),
        in_specs=[pl.BlockSpec((part, rows, own), lambda r: (r, 0, 0))] * 2
        + [pl.BlockSpec((own, width), lambda r: (0, 0))] * 2,
        out_specs=pl.BlockSpec((part, rows, width), lambda r: (r, 0, 0)),
        compiler_params=pltpu.CompilerParams(vmem_limit_bytes=VMEM),
        cost_estimate=pl.CostEstimate(
            flops=2 * seqs * rows * width * width,
            bytes_accessed=4 * seqs * rows * width + 2 * width * width,
            transcendentals=0,
        ),
        name="finish",
    )(mine, theirs, weight_mine, weight_theirs)


def ring_table(axis_of):
    return [
        (c * SIZE["x"] + i, c * SIZE["x"] + (i + (1 if c == axis_of else -1)) % SIZE["x"])
        for c in range(2)
        for i in range(SIZE["x"])
    ]


def send_x(arr, way):
    return lax.ppermute(arr, ("core", "x"), ring_table(way))


def per_device(data, query_matrix, key_matrix, value_matrix, output_matrix):
    seqs, rows, width = data.shape
    place = jnp.stack([lax.axis_index(a) for a in ("core", "y", "z_hi", "z_lo")])
    place = place.astype(jnp.int32)

    core = lax.axis_index("core")
    half = width // 2

    def swap(arr):
        return shift(arr, "core", 1)

    output_mine, output_theirs = (
        lax.dynamic_slice_in_dim(output_matrix, c * half, half, 0) for c in (core, 1 - core)
    )

    pairs, span, group = HEADS // 4, 4 * seqs * HEAD, rows // PARTS
    heads, v_shape = 2 * pairs, (pairs, rows, span)
    q_shape, k_shape = (heads, PARTS, group, span // 2), (heads, rows, span // 2)
    qa_shape, ka_shape = (*q_shape[:-1], span // 4), (*k_shape[:-1], span // 4)
    w_shape = (2, width, half)
    dma = pltpu.SemaphoreType.DMA

    def logits_shape(n):
        return jax.ShapeDtypeStruct((2, pairs, 2 * group, n * rows), BF16)

    def bf(*shape):
        return pltpu.VMEM(shape, BF16)

    first, second = send_x(data, 0), send_x(data, 1)
    partner = shift(data, "z_lo", 1)
    queries, keys, values, query_pair, key_pair = manual(
        own_body,
        place,
        [data, swap(data), query_matrix, key_matrix, value_matrix],
        [jax.ShapeDtypeStruct(s, BF16) for s in (q_shape, k_shape, v_shape, w_shape, w_shape)],
        [bf(2, *data.shape), bf(3, width, half), bf(*q_shape), bf(*k_shape), bf(*v_shape)]
        + [bf(2, *w_shape), dma((5,)), dma((5,))],
        12 * seqs * rows * width * half,
        "own",
    )
    first, second, partner = (tie([a], queries)[0] for a in (first, second, partner))
    near = [(first, swap(second)), (second, swap(first))]
    partner2 = (partner, swap(partner))
    def of(*shapes):
        return [jax.ShapeDtypeStruct(s, BF16) for s in shapes]

    work = 4 * seqs * rows * width * half
    qa, ka1, ka2 = local(
        near_body,
        place,
        [first, second, partner, query_pair, key_pair],
        of(qa_shape, ka_shape, ka_shape),
        3 * work // 2,
        "near",
    )
    k1, k2 = local(
        near_keys_body,
        place,
        [ka1, ka2, near[0][1], near[1][1], key_pair],
        of(k_shape, k_shape),
        work,
        "near_keys",
    )
    far_keys = send_x(k1, 0)
    qb, *near_logits = local(
        near_logits_body,
        place,
        [queries, qa, keys, k1, k2, partner2[1], query_pair],
        of(qa_shape) + [logits_shape(3)] * PARTS,
        2 * work,
        "near_logits",
    )
    (z_own,) = local(
        values_body,
        place,
        [*partner2, value_matrix],
        of(v_shape),
        work,
        "values_partner",
        [qb],
    )
    z_first, z_second = send_x(z_own, 0), send_x(z_own, 1)
    far_logits = local(
        far_logits_body,
        place,
        [queries, qa, qb, far_keys],
        [logits_shape(1)] * PARTS,
        work // 2,
        "far_logits",
        [z_own],
    )
    def over_y(parts):
        parts = [a.reshape(2, -1, a.shape[-1]) for a in parts]
        return [parts[0]] + [shift(parts[d], "y", d) for d in range(1, PARTS)]

    groups = [over_y(near_logits), over_y(far_logits)]
    sent = add_parts(place, groups)
    both_values, second_values = local(
        near_values_body,
        place,
        [*near[0], *near[1], z_first, value_matrix],
        of((2, *v_shape), v_shape),
        2 * work,
        "values_near",
        [sent],
    )
    sent = sent.reshape(2 * PARTS, *sent.shape[2:])
    got = lax.all_to_all(sent, ("z_hi", "z_lo"), 0, 0, tiled=True)
    got = got.reshape(PARTS, 2, *got.shape[1:])
    all_rows = seqs * lax.axis_size(("z_hi", "y", "core"))
    scale = HEAD ** (-0.5) * all_rows ** (-0.5)
    probs, z_second, both_values = softmax(place, got, scale, [z_second, both_values])
    far_values = send_x(both_values, 0)
    probs = order(place, [probs] + [shift(probs, "z_hi", d) for d in range(1, PARTS)])
    probs = probs.reshape(pairs, 2 * group, probs.shape[-1])
    parts = [values, both_values, second_values, far_values, z_own, z_second]
    (values,) = local(gather_body, place, parts, of((pairs, 8 * rows, span)), 0, "gather_values")
    probs = [probs] + [shift(probs, "y", d) for d in range(1, PARTS)]
    mine, theirs = mix(place, probs, values, seqs)
    return finish(mine, swap(theirs), output_mine, output_theirs)


def solution(mesh):
    fine = Mesh(mesh.devices.reshape(SIZES), AXES)
    spec = P(("z_hi", "y", "core"), ("x", "z_lo"), None)
    return jax.shard_map(
        per_device,
        mesh=fine,
        in_specs=(spec, P(), P(), P(), P()),
        out_specs=spec,
        check_vma=False,
    )
```

```python
import functools

import jax
import jax.numpy as jnp
from jax import lax
from jax.experimental import pallas as pl
from jax.experimental.pallas import tpu as pltpu
from jax.sharding import Mesh, PartitionSpec as P

HEADS = 12
HEAD = 64
AXES = ("z_hi", "y", "core", "x", "z_lo")
SIZES = (4, 4, 2, 4, 2)
SIZE = dict(zip(AXES, SIZES))
BF16 = jnp.bfloat16
F32 = jnp.float32
PARTS = 4
VMEM = 16 << 20


def shift(arr, axis, step):
    n = SIZE[axis]
    return lax.ppermute(arr, axis, [(i, (i + step) % n) for i in range(n)])


def whole(shape):
    return pl.BlockSpec(shape, lambda *_: (0,) * len(shape), pipeline_mode=pl.Buffered(1))


def call(body, place, ins, in_specs, outs, out_specs, grid, flops, name, late=()):
    moved = sum(a.size * a.dtype.itemsize for a in ins)
    moved += sum(o.size * o.dtype.itemsize for o in outs)
    n = 1 + len(ins)

    def run(*refs):
        body(*refs[:n], *refs[n + len(late) :])

    in_specs = [*in_specs] + [pl.BlockSpec(memory_space=pl.ANY)] * len(late)
    return pl.pallas_call(
        run,
        out_shape=outs,
        grid_spec=pltpu.PrefetchScalarGridSpec(
            num_scalar_prefetch=1, grid=grid, in_specs=in_specs, out_specs=out_specs
        ),
        compiler_params=pltpu.CompilerParams(vmem_limit_bytes=VMEM),
        cost_estimate=pl.CostEstimate(flops=flops, bytes_accessed=moved, transcendentals=0),
        name=name,
    )(place, *ins, *late)


def tie(arrays, late):
    n = len(arrays)
    free = pl.BlockSpec(memory_space=pl.ANY)
    return pl.pallas_call(
        lambda *refs: None,
        out_shape=[jax.ShapeDtypeStruct(a.shape, a.dtype) for a in arrays],
        in_specs=[free] * (n + 1),
        out_specs=[free] * n,
        input_output_aliases={i: i for i in range(n)},
        compiler_params=pltpu.CompilerParams(vmem_limit_bytes=1 << 20),
        name="tie",
    )(*arrays, late)


def rel(index):
    return lax.rem(index + PARTS, PARTS)


def manual(body, place, ins, outs, scratch, flops, name, late=()):
    moved = sum(a.size * a.dtype.itemsize for a in ins)
    moved += sum(o.size * o.dtype.itemsize for o in outs)
    n = 1 + len(ins)
    far_off = pl.BlockSpec(memory_space=pltpu.HBM)

    def run(*refs):
        body(*refs[:n], *refs[n + len(late) :])

    return pl.pallas_call(
        run,
        out_shape=outs,
        in_specs=[pl.BlockSpec(memory_space=pltpu.SMEM)]
        + [far_off] * len(ins)
        + [pl.BlockSpec(memory_space=pl.ANY)] * len(late),
        out_specs=[far_off] * len(outs),
        scratch_shapes=scratch,
        compiler_params=pltpu.CompilerParams(vmem_limit_bytes=VMEM),
        cost_estimate=pl.CostEstimate(flops=flops, bytes_accessed=moved, transcendentals=0),
        name=name,
    )(place, *ins, *late)


def local(body, place, ins, outs, flops, name, late=()):
    here = pl.BlockSpec(memory_space=pltpu.VMEM)
    moved = sum(a.size * a.dtype.itemsize for a in ins)
    moved += sum(o.size * o.dtype.itemsize for o in outs)
    n = 1 + len(ins)

    def run(*refs):
        body(*refs[:n], *refs[n + len(late) :])

    return pl.pallas_call(
        run,
        out_shape=outs,
        in_specs=[pl.BlockSpec(memory_space=pltpu.SMEM)] + [here] * len(ins)
        + [pl.BlockSpec(memory_space=pl.ANY)] * len(late),
        out_specs=[here] * len(outs),
        compiler_params=pltpu.CompilerParams(vmem_limit_bytes=VMEM),
        cost_estimate=pl.CostEstimate(flops=flops, bytes_accessed=moved, transcendentals=0),
        name=name,
    )(place, *ins, *late)


def start(src, dst, sem):
    copy = pltpu.make_async_copy(src, dst, sem)
    copy.start()
    return copy


def columns(weight, place):
    own = weight.shape[1] // 2
    return weight.at[:, pl.ds(pl.multiple_of(place[0] * own, own), own)]


def project(x_ref, half, weight, out, place):
    seqs, rows, width = x_ref.shape
    lanes = 2 * HEAD
    got = jnp.dot(
        x_ref[...].reshape(seqs * rows, width), weight[...], preferred_element_type=F32
    ).astype(BF16)
    for s in range(seqs):
        at = (half * seqs + s) * lanes
        for p in range(out.shape[0]):
            out[p, :, at : at + lanes] = got[s * rows : (s + 1) * rows, p * lanes : (p + 1) * lanes]


def project_heads(x_ref, half, weights, out, place):
    seqs, rows, width = x_ref.shape
    lanes, some = 2 * HEAD, seqs // 2
    group = rows // PARTS
    sides = [
        jnp.dot(
            x_ref[i * some : (i + 1) * some].reshape(some * rows, width),
            weights[i],
            preferred_element_type=F32,
        ).astype(BF16)
        for i in range(2)
    ]
    first = lax.broadcasted_iota(jnp.int32, (rows, lanes), 1) < HEAD
    for s in range(some):
        at = (half * some + s) * lanes
        for p in range(out.shape[0] // 2):
            one, two = (a[s * rows : (s + 1) * rows, p * lanes : (p + 1) * lanes] for a in sides)
            for h in range(2):
                part = jnp.where(first, two, one) if h else jnp.where(first, one, two)
                if len(out.shape) == 3:
                    out[2 * p + h, :, at : at + lanes] = part
                    continue
                for a in range(PARTS):
                    out[2 * p + h, rel(a - place[1]), :, at : at + lanes] = part[
                        a * group : (a + 1) * group
                    ]


def write_logits(queries, keys, outs):
    group = outs[0].shape[2] // 2
    for head in range(keys[0].shape[0]):
        k = jnp.concatenate([ref[head] for ref in keys], axis=0)
        q = jnp.concatenate(
            [
                jnp.concatenate([ref[head].reshape(PARTS * group, -1) for ref in refs], axis=-1)
                for refs in queries
            ],
            axis=0,
        )
        got = lax.dot_general(q, k, (((1,), (1,)), ((), ())), preferred_element_type=F32)
        at = head % 2 * group
        for i in range(len(queries)):
            for d, out in enumerate(outs):
                out[i, head // 2, at : at + group] = got[
                    (i * PARTS + d) * group : (i * PARTS + d + 1) * group
                ].astype(BF16)


def wait_all(copies):
    for copy in copies:
        copy.wait()


def own_body(place, x0, x1, wq, wk, wv, oq, ok, ov, oqw, okw, bx, bw, bq, bk, bv, bs, ins, outs):
    loads = [start(x, bx.at[i], ins.at[i]) for i, x in enumerate((x0, x1))]
    loads += [start(columns(w, place), bw.at[i], ins.at[2 + i]) for i, w in enumerate((wq, wk, wv))]
    lanes = 2 * HEAD
    stores = []
    for i, out in enumerate((oqw, okw)):
        loads[2 + i].wait()
        bs[i, 0] = bw[i]
        for p in range(bw.shape[2] // lanes):
            at = slice(p * lanes, (p + 1) * lanes)
            bs[i, 1, :, at] = pltpu.roll(bw[i, :, at].astype(F32), HEAD, 1).astype(BF16)
        stores.append(start(bs.at[i], out, outs.at[3 + i]))
    for load in loads[:2]:
        load.wait()
    for i, (out, held) in enumerate(((oq, bq), (ok, bk))):
        for half in range(2):
            project_heads(bx.at[half], half, bs.at[i], held, place)
        stores.append(start(held, out, outs.at[i]))
    loads[4].wait()
    for half in range(2):
        project(bx.at[half], half, bw.at[2], bv, place)
    stores.append(start(bv, ov, outs.at[2]))
    wait_all(stores)


def near_body(place, first, second, partner, wq, wk, qa, k1, k2):
    project_heads(first, 0, wk, k1, place)
    project_heads(second, 0, wk, k2, place)
    project_heads(partner, 0, wq, qa, place)


def near_keys_body(place, a1, a2, first, second, wk, k1, k2):
    half = a1.shape[2]
    for a, x, k in ((a1, first, k1), (a2, second, k2)):
        k[:, :, :half] = a[...]
        project_heads(x, 1, wk, k, place)


def near_logits_body(place, q0, qa, k0, k1, k2, partner, wq, qb, *outs):
    project_heads(partner, 0, wq, qb, place)
    write_logits([[q0], [qa, qb]], [k0, k1, k2], outs)


def far_logits_body(place, q0, qa, qb, k, *outs):
    write_logits([[q0], [qa, qb]], [k], outs)


def values_body(place, *refs):
    *xs, weight = refs[: len(refs) * 2 // 3 + 1]
    for i, out in enumerate(refs[len(xs) + 1 :]):
        for half in range(2):
            project(xs[2 * i + half], half, columns(weight, place), out, place)


def near_values_body(place, x0, x1, x2, x3, z_first, weight, both, second):
    for half, x in enumerate((x0, x1)):
        project(x, half, columns(weight, place), both.at[0], place)
    for half, x in enumerate((x2, x3)):
        project(x, half, columns(weight, place), second, place)
    both[1] = z_first[...]


def gather_body(place, own, both, second, far, z_own, z_second, out):
    blocks = (own, both.at[0], second, far.at[0], z_own, both.at[1], z_second, far.at[1])
    rows = own.shape[1]
    for i, ref in enumerate(blocks):
        out[:, i * rows : (i + 1) * rows, :] = ref[...]


def add_body(count, place, *refs):
    out, parts = refs[-1], refs[:-1]
    z_lo = place[3]
    sums = []
    for n in range(0, len(parts), count):
        total = parts[n][...].astype(F32)
        for ref in parts[n + 1 : n + count]:
            total += ref[...].astype(F32)
        sums.append(total)
    total = jnp.concatenate(sums, axis=-1).astype(BF16)
    share = out.shape[2]
    for i in range(2):
        for z in range(PARTS):
            out[z, i ^ z_lo] = total[i, z * share : (z + 1) * share]


def add_parts(place, groups):
    parts = [a for g in groups for a in g]
    rows = parts[0].shape[1]
    cols = sum(g[0].shape[2] for g in groups)
    return local(
        functools.partial(add_body, PARTS),
        place,
        parts,
        [jax.ShapeDtypeStruct((PARTS, 2, rows // PARTS, cols), BF16)],
        sum(a.size for a in parts),
        "add_over_y",
    )[0]


def softmax_body(scale, place, parts, *refs):
    out = refs[len(refs) // 2]
    z_lo = place[3]
    sides = []
    for side in (z_lo, 1 - z_lo):
        total = parts[0, side].astype(F32)
        for z in range(1, PARTS):
            total += parts[z, side].astype(F32)
        sides.append(total)
    scaled = jnp.concatenate(sides, axis=-1) * scale
    expo = jnp.exp(scaled - jnp.max(scaled, axis=-1, keepdims=True))
    out[...] = (expo / jnp.sum(expo, axis=-1, keepdims=True)).astype(BF16)


def softmax(place, parts, scale, others):
    shape = (parts.shape[2], 2 * parts.shape[3])
    free = [pl.BlockSpec(memory_space=pl.ANY)] * len(others)
    here = pl.BlockSpec(memory_space=pltpu.VMEM)
    return pl.pallas_call(
        functools.partial(softmax_body, scale),
        out_shape=[jax.ShapeDtypeStruct(shape, BF16)]
        + [jax.ShapeDtypeStruct(a.shape, a.dtype) for a in others],
        in_specs=[pl.BlockSpec(memory_space=pltpu.SMEM), here, *free],
        out_specs=[here, *free],
        input_output_aliases={2 + i: 1 + i for i in range(len(others))},
        compiler_params=pltpu.CompilerParams(vmem_limit_bytes=VMEM),
        cost_estimate=pl.CostEstimate(
            flops=parts.size * 8, bytes_accessed=parts.size * 4, transcendentals=parts.size // 4
        ),
        name="softmax",
    )(place, parts, *others)


def order_body(place, *refs):
    out, parts = refs[-1], refs[:-1]
    for d, ref in enumerate(parts):
        out[rel(place[2] - d)] = ref[...]


def order(place, parts):
    shape = (PARTS, *parts[0].shape)
    return call(
        order_body,
        place,
        parts,
        [whole(a.shape) for a in parts],
        [jax.ShapeDtypeStruct(shape, BF16)],
        [whole(shape)],
        (1,),
        0,
        "order",
    )[0]


def mix_body(place, *refs):
    probs, values, outs = refs[:PARTS], refs[PARTS], refs[-2:]
    y = place[1]
    pairs, half, _ = probs[0].shape
    group = half // 2
    lanes = 2 * HEAD
    seqs = outs[0].shape[0]
    first = lax.broadcasted_iota(jnp.int32, (group, lanes), 1) < HEAD
    for pair in range(pairs):
        p = jnp.concatenate([ref[pair] for ref in probs], axis=0)
        got = jnp.dot(p, values[pair], preferred_element_type=F32)
        for d in range(PARTS):
            at = pl.multiple_of(rel(y - d) * group, group)
            for s in range(2 * seqs):
                one, two = (
                    got[(2 * d + h) * group : (2 * d + h + 1) * group, s * lanes : (s + 1) * lanes]
                    for h in range(2)
                )
                outs[s // seqs][
                    s % seqs, pl.ds(at, group), pair * lanes : (pair + 1) * lanes
                ] = jnp.where(first, one, two).astype(BF16)


def mix(place, probs, values, seqs):
    pairs, half, cols = probs[0].shape
    rows = PARTS * half // 2
    return local(
        mix_body,
        place,
        [*probs, values],
        [jax.ShapeDtypeStruct((seqs, rows, pairs * 2 * HEAD), BF16)] * 2,
        2 * pairs * PARTS * half * cols * values.shape[2],
        "mix",
    )


def finish_body(mine, theirs, weight_mine, weight_theirs, out):
    seqs, rows, own = mine.shape
    got = jnp.dot(mine[...].reshape(seqs * rows, own), weight_mine[...], preferred_element_type=F32)
    got += jnp.dot(
        theirs[...].reshape(seqs * rows, own), weight_theirs[...], preferred_element_type=F32
    )
    out[...] = got.astype(BF16).reshape(out.shape)


def finish(mine, theirs, weight_mine, weight_theirs):
    seqs, rows, own = mine.shape
    width = weight_mine.shape[1]
    part = seqs // 2
    return pl.pallas_call(
        finish_body,
        out_shape=jax.ShapeDtypeStruct((seqs, rows, width), BF16),
        grid=(seqs // part,),
        in_specs=[pl.BlockSpec((part, rows, own), lambda r: (r, 0, 0))] * 2
        + [pl.BlockSpec((own, width), lambda r: (0, 0))] * 2,
        out_specs=pl.BlockSpec((part, rows, width), lambda r: (r, 0, 0)),
        compiler_params=pltpu.CompilerParams(vmem_limit_bytes=VMEM),
        cost_estimate=pl.CostEstimate(
            flops=2 * seqs * rows * width * width,
            bytes_accessed=4 * seqs * rows * width + 2 * width * width,
            transcendentals=0,
        ),
        name="finish",
    )(mine, theirs, weight_mine, weight_theirs)


def ring_table(axis_of):
    return [
        (c * SIZE["x"] + i, c * SIZE["x"] + (i + (1 if c == axis_of else -1)) % SIZE["x"])
        for c in range(2)
        for i in range(SIZE["x"])
    ]


def send_x(arr, way):
    return lax.ppermute(arr, ("core", "x"), ring_table(way))


def send_y(arr, way):
    table = [
        (i * 2 + c, (i + (1 if c == way else -1)) % PARTS * 2 + c) for i in range(PARTS) for c in range(2)
    ]
    return lax.ppermute(arr, ("y", "core"), table)


def per_device(data, query_matrix, key_matrix, value_matrix, output_matrix):
    seqs, rows, width = data.shape
    place = jnp.stack([lax.axis_index(a) for a in ("core", "y", "z_hi", "z_lo")])
    place = place.astype(jnp.int32)

    core = lax.axis_index("core")
    half = width // 2

    def swap(arr):
        return shift(arr, "core", 1)

    output_mine, output_theirs = (
        lax.dynamic_slice_in_dim(output_matrix, c * half, half, 0) for c in (core, 1 - core)
    )

    pairs, span, group = HEADS // 4, 4 * seqs * HEAD, rows // PARTS
    heads, v_shape = 2 * pairs, (pairs, rows, span)
    q_shape, k_shape = (heads, PARTS, group, span // 2), (heads, rows, span // 2)
    qa_shape, ka_shape = (*q_shape[:-1], span // 4), (*k_shape[:-1], span // 4)
    w_shape = (2, width, half)
    dma = pltpu.SemaphoreType.DMA

    def logits_shape(n):
        return jax.ShapeDtypeStruct((2, pairs, 2 * group, n * rows), BF16)

    def bf(*shape):
        return pltpu.VMEM(shape, BF16)

    first, second = send_x(data, 0), send_x(data, 1)
    partner = shift(data, "z_lo", 1)
    queries, keys, values, query_pair, key_pair = manual(
        own_body,
        place,
        [data, swap(data), query_matrix, key_matrix, value_matrix],
        [jax.ShapeDtypeStruct(s, BF16) for s in (q_shape, k_shape, v_shape, w_shape, w_shape)],
        [bf(2, *data.shape), bf(3, width, half), bf(*q_shape), bf(*k_shape), bf(*v_shape)]
        + [bf(2, *w_shape), dma((5,)), dma((5,))],
        12 * seqs * rows * width * half,
        "own",
    )
    first, second, partner = (tie([a], queries)[0] for a in (first, second, partner))
    near = [(first, swap(second)), (second, swap(first))]
    partner2 = (partner, swap(partner))
    def of(*shapes):
        return [jax.ShapeDtypeStruct(s, BF16) for s in shapes]

    work = 4 * seqs * rows * width * half
    qa, ka1, ka2 = local(
        near_body,
        place,
        [first, second, partner, query_pair, key_pair],
        of(qa_shape, ka_shape, ka_shape),
        3 * work // 2,
        "near",
    )
    k1, k2 = local(
        near_keys_body,
        place,
        [ka1, ka2, near[0][1], near[1][1], key_pair],
        of(k_shape, k_shape),
        work,
        "near_keys",
    )
    far_keys = send_x(k1, 0)
    qb, *near_logits = local(
        near_logits_body,
        place,
        [queries, qa, keys, k1, k2, partner2[1], query_pair],
        of(qa_shape) + [logits_shape(3)] * PARTS,
        2 * work,
        "near_logits",
    )
    (z_own,) = local(
        values_body,
        place,
        [*partner2, value_matrix],
        of(v_shape),
        work,
        "values_partner",
        [qb],
    )
    far_logits = local(
        far_logits_body,
        place,
        [queries, qa, qb, far_keys],
        [logits_shape(1)] * PARTS,
        work // 2,
        "far_logits",
        [z_own],
    )
    (z_own,) = tie([z_own], far_logits[0])
    z_first, z_second = send_x(z_own, 0), send_x(z_own, 1)

    def over_y(parts, split):
        parts = [a.reshape(2, -1, a.shape[-1]) for a in parts]
        if split:
            (opposite,) = tie([send_y(parts[2], 0)], z_own)
            opposite = send_y(opposite, 0)
        else:
            opposite = shift(parts[2], "y", 2)
        return [parts[0], shift(parts[1], "y", 1), opposite, shift(parts[3], "y", 3)]

    groups = [over_y(near_logits, True), over_y(far_logits, False)]
    sent = add_parts(place, groups)
    both_values, second_values = local(
        near_values_body,
        place,
        [*near[0], *near[1], z_first, value_matrix],
        of((2, *v_shape), v_shape),
        2 * work,
        "values_near",
        [sent],
    )
    sent = sent.reshape(2 * PARTS, *sent.shape[2:])
    got = lax.all_to_all(sent, ("z_hi", "z_lo"), 0, 0, tiled=True)
    got = got.reshape(PARTS, 2, *got.shape[1:])
    all_rows = seqs * lax.axis_size(("z_hi", "y", "core"))
    scale = HEAD ** (-0.5) * all_rows ** (-0.5)
    probs, z_second, both_values = softmax(place, got, scale, [z_second, both_values])
    far_values = send_x(both_values, 0)
    probs = order(place, [probs] + [shift(probs, "z_hi", d) for d in range(1, PARTS)])
    probs = probs.reshape(pairs, 2 * group, probs.shape[-1])
    parts = [values, both_values, second_values, far_values, z_own, z_second]
    (values,) = local(gather_body, place, parts, of((pairs, 8 * rows, span)), 0, "gather_values")
    probs = [probs] + [shift(probs, "y", d) for d in range(1, PARTS)]
    mine, theirs = mix(place, probs, values, seqs)
    return finish(mine, swap(theirs), output_mine, output_theirs)


def solution(mesh):
    fine = Mesh(mesh.devices.reshape(SIZES), AXES)
    spec = P(("z_hi", "y", "core"), ("x", "z_lo"), None)
    return jax.shard_map(
        per_device,
        mesh=fine,
        in_specs=(spec, P(), P(), P(), P()),
        out_specs=spec,
        check_vma=False,
    )
```

```python
import functools

import jax
import jax.numpy as jnp
from jax import lax
from jax.experimental import pallas as pl
from jax.experimental.pallas import tpu as pltpu
from jax.sharding import Mesh, PartitionSpec as P

HEADS = 12
HEAD = 64
AXES = ("z_hi", "y", "core", "x", "z_lo")
SIZES = (4, 4, 2, 4, 2)
SIZE = dict(zip(AXES, SIZES))
BF16 = jnp.bfloat16
F32 = jnp.float32
PARTS = 4
VMEM = 16 << 20


def shift(arr, axis, step):
    n = SIZE[axis]
    return lax.ppermute(arr, axis, [(i, (i + step) % n) for i in range(n)])


def whole(shape):
    return pl.BlockSpec(shape, lambda *_: (0,) * len(shape), pipeline_mode=pl.Buffered(1))


def call(body, place, ins, in_specs, outs, out_specs, grid, flops, name, late=()):
    moved = sum(a.size * a.dtype.itemsize for a in ins)
    moved += sum(o.size * o.dtype.itemsize for o in outs)
    n = 1 + len(ins)

    def run(*refs):
        body(*refs[:n], *refs[n + len(late) :])

    in_specs = [*in_specs] + [pl.BlockSpec(memory_space=pl.ANY)] * len(late)
    return pl.pallas_call(
        run,
        out_shape=outs,
        grid_spec=pltpu.PrefetchScalarGridSpec(
            num_scalar_prefetch=1, grid=grid, in_specs=in_specs, out_specs=out_specs
        ),
        compiler_params=pltpu.CompilerParams(vmem_limit_bytes=VMEM),
        cost_estimate=pl.CostEstimate(flops=flops, bytes_accessed=moved, transcendentals=0),
        name=name,
    )(place, *ins, *late)


def tie(arrays, late):
    n = len(arrays)
    free = pl.BlockSpec(memory_space=pl.ANY)
    return pl.pallas_call(
        lambda *refs: None,
        out_shape=[jax.ShapeDtypeStruct(a.shape, a.dtype) for a in arrays],
        in_specs=[free] * (n + 1),
        out_specs=[free] * n,
        input_output_aliases={i: i for i in range(n)},
        compiler_params=pltpu.CompilerParams(vmem_limit_bytes=1 << 20),
        name="tie",
    )(*arrays, late)


def rel(index):
    return lax.rem(index + PARTS, PARTS)


def manual(body, place, ins, outs, scratch, flops, name, late=()):
    moved = sum(a.size * a.dtype.itemsize for a in ins)
    moved += sum(o.size * o.dtype.itemsize for o in outs)
    n = 1 + len(ins)
    far_off = pl.BlockSpec(memory_space=pltpu.HBM)

    def run(*refs):
        body(*refs[:n], *refs[n + len(late) :])

    return pl.pallas_call(
        run,
        out_shape=outs,
        in_specs=[pl.BlockSpec(memory_space=pltpu.SMEM)]
        + [far_off] * len(ins)
        + [pl.BlockSpec(memory_space=pl.ANY)] * len(late),
        out_specs=[far_off] * len(outs),
        scratch_shapes=scratch,
        compiler_params=pltpu.CompilerParams(vmem_limit_bytes=VMEM),
        cost_estimate=pl.CostEstimate(flops=flops, bytes_accessed=moved, transcendentals=0),
        name=name,
    )(place, *ins, *late)


def local(body, place, ins, outs, flops, name, late=()):
    here = pl.BlockSpec(memory_space=pltpu.VMEM)
    moved = sum(a.size * a.dtype.itemsize for a in ins)
    moved += sum(o.size * o.dtype.itemsize for o in outs)
    n = 1 + len(ins)

    def run(*refs):
        body(*refs[:n], *refs[n + len(late) :])

    return pl.pallas_call(
        run,
        out_shape=outs,
        in_specs=[pl.BlockSpec(memory_space=pltpu.SMEM)] + [here] * len(ins)
        + [pl.BlockSpec(memory_space=pl.ANY)] * len(late),
        out_specs=[here] * len(outs),
        compiler_params=pltpu.CompilerParams(vmem_limit_bytes=VMEM),
        cost_estimate=pl.CostEstimate(flops=flops, bytes_accessed=moved, transcendentals=0),
        name=name,
    )(place, *ins, *late)


def start(src, dst, sem):
    copy = pltpu.make_async_copy(src, dst, sem)
    copy.start()
    return copy


def columns(weight, place):
    own = weight.shape[1] // 2
    return weight.at[:, pl.ds(pl.multiple_of(place[0] * own, own), own)]


def project(x_ref, half, weight, out, place):
    seqs, rows, width = x_ref.shape
    lanes = 2 * HEAD
    got = jnp.dot(
        x_ref[...].reshape(seqs * rows, width), weight[...], preferred_element_type=F32
    ).astype(BF16)
    for s in range(seqs):
        at = (half * seqs + s) * lanes
        for p in range(out.shape[0]):
            out[p, :, at : at + lanes] = got[s * rows : (s + 1) * rows, p * lanes : (p + 1) * lanes]


def project_heads(x_ref, half, weights, out, place):
    seqs, rows, width = x_ref.shape
    lanes, some = 2 * HEAD, seqs // 2
    group = rows // PARTS
    sides = [
        jnp.dot(
            x_ref[i * some : (i + 1) * some].reshape(some * rows, width),
            weights[i],
            preferred_element_type=F32,
        ).astype(BF16)
        for i in range(2)
    ]
    first = lax.broadcasted_iota(jnp.int32, (rows, lanes), 1) < HEAD
    for s in range(some):
        at = (half * some + s) * lanes
        for p in range(out.shape[0] // 2):
            one, two = (a[s * rows : (s + 1) * rows, p * lanes : (p + 1) * lanes] for a in sides)
            for h in range(2):
                part = jnp.where(first, two, one) if h else jnp.where(first, one, two)
                if len(out.shape) == 3:
                    out[2 * p + h, :, at : at + lanes] = part
                    continue
                for a in range(PARTS):
                    out[2 * p + h, rel(a - place[1]), :, at : at + lanes] = part[
                        a * group : (a + 1) * group
                    ]


def write_logits(queries, keys, outs):
    group = outs[0].shape[2] // 2
    for head in range(keys[0].shape[0]):
        k = jnp.concatenate([ref[head] for ref in keys], axis=0)
        q = jnp.concatenate(
            [
                jnp.concatenate([ref[head].reshape(PARTS * group, -1) for ref in refs], axis=-1)
                for refs in queries
            ],
            axis=0,
        )
        got = lax.dot_general(q, k, (((1,), (1,)), ((), ())), preferred_element_type=F32)
        at = head % 2 * group
        for i in range(len(queries)):
            for d, out in enumerate(outs):
                out[i, head // 2, at : at + group] = got[
                    (i * PARTS + d) * group : (i * PARTS + d + 1) * group
                ].astype(BF16)


def wait_all(copies):
    for copy in copies:
        copy.wait()


def own_body(place, x0, x1, wq, wk, wv, oq, ok, ov, oqw, okw, bx, bw, bq, bk, bv, bs, ins, outs):
    loads = [start(x, bx.at[i], ins.at[i]) for i, x in enumerate((x0, x1))]
    loads += [start(columns(w, place), bw.at[i], ins.at[2 + i]) for i, w in enumerate((wq, wk, wv))]
    lanes = 2 * HEAD
    stores = []
    for i, out in enumerate((oqw, okw)):
        loads[2 + i].wait()
        bs[i, 0] = bw[i]
        for p in range(bw.shape[2] // lanes):
            at = slice(p * lanes, (p + 1) * lanes)
            bs[i, 1, :, at] = pltpu.roll(bw[i, :, at].astype(F32), HEAD, 1).astype(BF16)
        stores.append(start(bs.at[i], out, outs.at[3 + i]))
    for load in loads[:2]:
        load.wait()
    for i, (out, held) in enumerate(((oq, bq), (ok, bk))):
        for half in range(2):
            project_heads(bx.at[half], half, bs.at[i], held, place)
        stores.append(start(held, out, outs.at[i]))
    loads[4].wait()
    for half in range(2):
        project(bx.at[half], half, bw.at[2], bv, place)
    stores.append(start(bv, ov, outs.at[2]))
    wait_all(stores)


def near_body(place, first, second, partner, wq, wk, qa, k1, k2):
    project_heads(first, 0, wk, k1, place)
    project_heads(second, 0, wk, k2, place)
    project_heads(partner, 0, wq, qa, place)


def near_keys_body(place, a1, a2, first, second, wk, k1, k2):
    half = a1.shape[2]
    for a, x, k in ((a1, first, k1), (a2, second, k2)):
        k[:, :, :half] = a[...]
        project_heads(x, 1, wk, k, place)


def near_logits_body(place, q0, qa, k0, k1, k2, partner, wq, qb, *outs):
    project_heads(partner, 0, wq, qb, place)
    write_logits([[q0], [qa, qb]], [k0, k1, k2], outs)


def far_logits_body(place, q0, qa, qb, k, *outs):
    write_logits([[q0], [qa, qb]], [k], outs)


def values_body(place, *refs):
    *xs, weight = refs[: len(refs) * 2 // 3 + 1]
    for i, out in enumerate(refs[len(xs) + 1 :]):
        for half in range(2):
            project(xs[2 * i + half], half, columns(weight, place), out, place)


def near_values_body(place, x0, x1, x2, x3, z_first, weight, both, second):
    for half, x in enumerate((x0, x1)):
        project(x, half, columns(weight, place), both.at[0], place)
    for half, x in enumerate((x2, x3)):
        project(x, half, columns(weight, place), second, place)
    both[1] = z_first[...]


def gather_body(place, own, both, second, far, z_own, z_second, out):
    blocks = (own, both.at[0], second, far.at[0], z_own, both.at[1], z_second, far.at[1])
    rows = own.shape[1]
    for i, ref in enumerate(blocks):
        out[:, i * rows : (i + 1) * rows, :] = ref[...]


def add_body(count, place, *refs):
    out, parts = refs[-1], refs[:-1]
    z_lo = place[3]
    sums = []
    for n in range(0, len(parts), count):
        total = parts[n][...].astype(F32)
        for ref in parts[n + 1 : n + count]:
            total += ref[...].astype(F32)
        sums.append(total)
    total = jnp.concatenate(sums, axis=-1).astype(BF16)
    share = out.shape[2]
    for i in range(2):
        for z in range(PARTS):
            out[z, i ^ z_lo] = total[i, z * share : (z + 1) * share]


def add_parts(place, groups):
    parts = [a for g in groups for a in g]
    rows = parts[0].shape[1]
    cols = sum(g[0].shape[2] for g in groups)
    return local(
        functools.partial(add_body, PARTS),
        place,
        parts,
        [jax.ShapeDtypeStruct((PARTS, 2, rows // PARTS, cols), BF16)],
        sum(a.size for a in parts),
        "add_over_y",
    )[0]


def softmax_body(scale, place, parts, *refs):
    out = refs[len(refs) // 2]
    z_lo = place[3]
    sides = []
    for side in (z_lo, 1 - z_lo):
        total = parts[0, side].astype(F32)
        for z in range(1, PARTS):
            total += parts[z, side].astype(F32)
        sides.append(total)
    scaled = jnp.concatenate(sides, axis=-1) * scale
    expo = jnp.exp(scaled - jnp.max(scaled, axis=-1, keepdims=True))
    out[...] = (expo / jnp.sum(expo, axis=-1, keepdims=True)).astype(BF16)


def softmax(place, parts, scale, others):
    shape = (parts.shape[2], 2 * parts.shape[3])
    free = [pl.BlockSpec(memory_space=pl.ANY)] * len(others)
    here = pl.BlockSpec(memory_space=pltpu.VMEM)
    return pl.pallas_call(
        functools.partial(softmax_body, scale),
        out_shape=[jax.ShapeDtypeStruct(shape, BF16)]
        + [jax.ShapeDtypeStruct(a.shape, a.dtype) for a in others],
        in_specs=[pl.BlockSpec(memory_space=pltpu.SMEM), here, *free],
        out_specs=[here, *free],
        input_output_aliases={2 + i: 1 + i for i in range(len(others))},
        compiler_params=pltpu.CompilerParams(vmem_limit_bytes=VMEM),
        cost_estimate=pl.CostEstimate(
            flops=parts.size * 8, bytes_accessed=parts.size * 4, transcendentals=parts.size // 4
        ),
        name="softmax",
    )(place, parts, *others)


def order_body(place, *refs):
    out, parts = refs[-1], refs[:-1]
    for d, ref in enumerate(parts):
        out[rel(place[2] - d)] = ref[...]


def order(place, parts):
    shape = (PARTS, *parts[0].shape)
    return call(
        order_body,
        place,
        parts,
        [whole(a.shape) for a in parts],
        [jax.ShapeDtypeStruct(shape, BF16)],
        [whole(shape)],
        (1,),
        0,
        "order",
    )[0]


def mix_body(place, *refs):
    probs, values, outs = refs[:PARTS], refs[PARTS], refs[-2:]
    y = place[1]
    pairs, half, _ = probs[0].shape
    group = half // 2
    lanes = 2 * HEAD
    seqs = outs[0].shape[0]
    first = lax.broadcasted_iota(jnp.int32, (group, lanes), 1) < HEAD
    for pair in range(pairs):
        p = jnp.concatenate([ref[pair] for ref in probs], axis=0)
        got = jnp.dot(p, values[pair], preferred_element_type=F32)
        for d, step in enumerate((0, 1 - 2 * place[0], 2 * place[0] - 1, 2)):
            at = pl.multiple_of(rel(y - step) * group, group)
            for s in range(2 * seqs):
                one, two = (
                    got[(2 * d + h) * group : (2 * d + h + 1) * group, s * lanes : (s + 1) * lanes]
                    for h in range(2)
                )
                outs[s // seqs][
                    s % seqs, pl.ds(at, group), pair * lanes : (pair + 1) * lanes
                ] = jnp.where(first, one, two).astype(BF16)


def mix(place, probs, values, seqs):
    pairs, half, cols = probs[0].shape
    rows = PARTS * half // 2
    return local(
        mix_body,
        place,
        [*probs, values],
        [jax.ShapeDtypeStruct((seqs, rows, pairs * 2 * HEAD), BF16)] * 2,
        2 * pairs * PARTS * half * cols * values.shape[2],
        "mix",
    )


def finish_body(mine, theirs, weight_mine, weight_theirs, out):
    seqs, rows, own = mine.shape
    got = jnp.dot(mine[...].reshape(seqs * rows, own), weight_mine[...], preferred_element_type=F32)
    got += jnp.dot(
        theirs[...].reshape(seqs * rows, own), weight_theirs[...], preferred_element_type=F32
    )
    out[...] = got.astype(BF16).reshape(out.shape)


def finish(mine, theirs, weight_mine, weight_theirs):
    seqs, rows, own = mine.shape
    width = weight_mine.shape[1]
    part = seqs // 2
    return pl.pallas_call(
        finish_body,
        out_shape=jax.ShapeDtypeStruct((seqs, rows, width), BF16),
        grid=(seqs // part,),
        in_specs=[pl.BlockSpec((part, rows, own), lambda r: (r, 0, 0))] * 2
        + [pl.BlockSpec((own, width), lambda r: (0, 0))] * 2,
        out_specs=pl.BlockSpec((part, rows, width), lambda r: (r, 0, 0)),
        compiler_params=pltpu.CompilerParams(vmem_limit_bytes=VMEM),
        cost_estimate=pl.CostEstimate(
            flops=2 * seqs * rows * width * width,
            bytes_accessed=4 * seqs * rows * width + 2 * width * width,
            transcendentals=0,
        ),
        name="finish",
    )(mine, theirs, weight_mine, weight_theirs)


def ring_table(axis_of):
    return [
        (c * SIZE["x"] + i, c * SIZE["x"] + (i + (1 if c == axis_of else -1)) % SIZE["x"])
        for c in range(2)
        for i in range(SIZE["x"])
    ]


def send_x(arr, way):
    return lax.ppermute(arr, ("core", "x"), ring_table(way))


def send_y(arr, way):
    table = [
        (i * 2 + c, (i + (1 if c == way else -1)) % PARTS * 2 + c) for i in range(PARTS) for c in range(2)
    ]
    return lax.ppermute(arr, ("y", "core"), table)


def per_device(data, query_matrix, key_matrix, value_matrix, output_matrix):
    seqs, rows, width = data.shape
    place = jnp.stack([lax.axis_index(a) for a in ("core", "y", "z_hi", "z_lo")])
    place = place.astype(jnp.int32)

    core = lax.axis_index("core")
    half = width // 2

    def swap(arr):
        return shift(arr, "core", 1)

    output_mine, output_theirs = (
        lax.dynamic_slice_in_dim(output_matrix, c * half, half, 0) for c in (core, 1 - core)
    )

    pairs, span, group = HEADS // 4, 4 * seqs * HEAD, rows // PARTS
    heads, v_shape = 2 * pairs, (pairs, rows, span)
    q_shape, k_shape = (heads, PARTS, group, span // 2), (heads, rows, span // 2)
    qa_shape, ka_shape = (*q_shape[:-1], span // 4), (*k_shape[:-1], span // 4)
    w_shape = (2, width, half)
    dma = pltpu.SemaphoreType.DMA

    def logits_shape(n):
        return jax.ShapeDtypeStruct((2, pairs, 2 * group, n * rows), BF16)

    def bf(*shape):
        return pltpu.VMEM(shape, BF16)

    first, second = send_x(data, 0), send_x(data, 1)
    partner = shift(data, "z_lo", 1)
    queries, keys, values, query_pair, key_pair = manual(
        own_body,
        place,
        [data, swap(data), query_matrix, key_matrix, value_matrix],
        [jax.ShapeDtypeStruct(s, BF16) for s in (q_shape, k_shape, v_shape, w_shape, w_shape)],
        [bf(2, *data.shape), bf(3, width, half), bf(*q_shape), bf(*k_shape), bf(*v_shape)]
        + [bf(2, *w_shape), dma((5,)), dma((5,))],
        12 * seqs * rows * width * half,
        "own",
    )
    first, second, partner = (tie([a], queries)[0] for a in (first, second, partner))
    near = [(first, swap(second)), (second, swap(first))]
    partner2 = (partner, swap(partner))
    def of(*shapes):
        return [jax.ShapeDtypeStruct(s, BF16) for s in shapes]

    work = 4 * seqs * rows * width * half
    qa, ka1, ka2 = local(
        near_body,
        place,
        [first, second, partner, query_pair, key_pair],
        of(qa_shape, ka_shape, ka_shape),
        3 * work // 2,
        "near",
    )
    k1, k2 = local(
        near_keys_body,
        place,
        [ka1, ka2, near[0][1], near[1][1], key_pair],
        of(k_shape, k_shape),
        work,
        "near_keys",
    )
    far_keys = send_x(k1, 0)
    qb, *near_logits = local(
        near_logits_body,
        place,
        [queries, qa, keys, k1, k2, partner2[1], query_pair],
        of(qa_shape) + [logits_shape(3)] * PARTS,
        2 * work,
        "near_logits",
    )
    (z_own,) = local(
        values_body,
        place,
        [*partner2, value_matrix],
        of(v_shape),
        work,
        "values_partner",
        [qb],
    )
    z_first, z_second = send_x(z_own, 0), send_x(z_own, 1)
    far_logits = local(
        far_logits_body,
        place,
        [queries, qa, qb, far_keys],
        [logits_shape(1)] * PARTS,
        work // 2,
        "far_logits",
        [z_own],
    )
    def over_y(parts):
        parts = [a.reshape(2, -1, a.shape[-1]) for a in parts]
        return [parts[0]] + [shift(parts[d], "y", d) for d in range(1, PARTS)]

    groups = [over_y(near_logits), over_y(far_logits)]
    sent = add_parts(place, groups)
    both_values, second_values = local(
        near_values_body,
        place,
        [*near[0], *near[1], z_first, value_matrix],
        of((2, *v_shape), v_shape),
        2 * work,
        "values_near",
        [sent],
    )
    sent = sent.reshape(2 * PARTS, *sent.shape[2:])
    got = lax.all_to_all(sent, ("z_hi", "z_lo"), 0, 0, tiled=True)
    got = got.reshape(PARTS, 2, *got.shape[1:])
    all_rows = seqs * lax.axis_size(("z_hi", "y", "core"))
    scale = HEAD ** (-0.5) * all_rows ** (-0.5)
    probs, z_second, both_values = softmax(place, got, scale, [z_second, both_values])
    far_values = send_x(both_values, 0)
    probs = order(place, [probs] + [shift(probs, "z_hi", d) for d in range(1, PARTS)])
    probs = probs.reshape(pairs, 2 * group, probs.shape[-1])
    parts = [values, both_values, second_values, far_values, z_own, z_second]
    (values,) = local(gather_body, place, parts, of((pairs, 8 * rows, span)), 0, "gather_values")
    probs = [probs, send_y(probs, 0), send_y(probs, 1)]
    probs.append(send_y(probs[1], 0))
    mine, theirs = mix(place, probs, values, seqs)
    return finish(mine, swap(theirs), output_mine, output_theirs)


def solution(mesh):
    fine = Mesh(mesh.devices.reshape(SIZES), AXES)
    spec = P(("z_hi", "y", "core"), ("x", "z_lo"), None)
    return jax.shard_map(
        per_device,
        mesh=fine,
        in_specs=(spec, P(), P(), P(), P()),
        out_specs=spec,
        check_vma=False,
    )
```

```python
import functools

import jax
import jax.numpy as jnp
from jax import lax
from jax.experimental import pallas as pl
from jax.experimental.pallas import tpu as pltpu
from jax.sharding import Mesh, PartitionSpec as P

HEADS = 12
HEAD = 64
AXES = ("z_hi", "y", "core", "x", "z_lo")
SIZES = (4, 4, 2, 4, 2)
SIZE = dict(zip(AXES, SIZES))
BF16 = jnp.bfloat16
F32 = jnp.float32
PARTS = 4
VMEM = 16 << 20


def shift(arr, axis, step):
    n = SIZE[axis]
    return lax.ppermute(arr, axis, [(i, (i + step) % n) for i in range(n)])


def whole(shape):
    return pl.BlockSpec(shape, lambda *_: (0,) * len(shape), pipeline_mode=pl.Buffered(1))


def call(body, place, ins, in_specs, outs, out_specs, grid, flops, name, late=()):
    moved = sum(a.size * a.dtype.itemsize for a in ins)
    moved += sum(o.size * o.dtype.itemsize for o in outs)
    n = 1 + len(ins)

    def run(*refs):
        body(*refs[:n], *refs[n + len(late) :])

    in_specs = [*in_specs] + [pl.BlockSpec(memory_space=pl.ANY)] * len(late)
    return pl.pallas_call(
        run,
        out_shape=outs,
        grid_spec=pltpu.PrefetchScalarGridSpec(
            num_scalar_prefetch=1, grid=grid, in_specs=in_specs, out_specs=out_specs
        ),
        compiler_params=pltpu.CompilerParams(vmem_limit_bytes=VMEM),
        cost_estimate=pl.CostEstimate(flops=flops, bytes_accessed=moved, transcendentals=0),
        name=name,
    )(place, *ins, *late)


def tie(arrays, late):
    n = len(arrays)
    free = pl.BlockSpec(memory_space=pl.ANY)
    return pl.pallas_call(
        lambda *refs: None,
        out_shape=[jax.ShapeDtypeStruct(a.shape, a.dtype) for a in arrays],
        in_specs=[free] * (n + 1),
        out_specs=[free] * n,
        input_output_aliases={i: i for i in range(n)},
        compiler_params=pltpu.CompilerParams(vmem_limit_bytes=1 << 20),
        name="tie",
    )(*arrays, late)


def rel(index):
    return lax.rem(index + PARTS, PARTS)


def manual(body, place, ins, outs, scratch, flops, name, late=()):
    moved = sum(a.size * a.dtype.itemsize for a in ins)
    moved += sum(o.size * o.dtype.itemsize for o in outs)
    n = 1 + len(ins)
    far_off = pl.BlockSpec(memory_space=pltpu.HBM)

    def run(*refs):
        body(*refs[:n], *refs[n + len(late) :])

    return pl.pallas_call(
        run,
        out_shape=outs,
        in_specs=[pl.BlockSpec(memory_space=pltpu.SMEM)]
        + [far_off] * len(ins)
        + [pl.BlockSpec(memory_space=pl.ANY)] * len(late),
        out_specs=[far_off] * len(outs),
        scratch_shapes=scratch,
        compiler_params=pltpu.CompilerParams(vmem_limit_bytes=VMEM),
        cost_estimate=pl.CostEstimate(flops=flops, bytes_accessed=moved, transcendentals=0),
        name=name,
    )(place, *ins, *late)


def local(body, place, ins, outs, flops, name, late=()):
    here = pl.BlockSpec(memory_space=pltpu.VMEM)
    moved = sum(a.size * a.dtype.itemsize for a in ins)
    moved += sum(o.size * o.dtype.itemsize for o in outs)
    n = 1 + len(ins)

    def run(*refs):
        body(*refs[:n], *refs[n + len(late) :])

    return pl.pallas_call(
        run,
        out_shape=outs,
        in_specs=[pl.BlockSpec(memory_space=pltpu.SMEM)] + [here] * len(ins)
        + [pl.BlockSpec(memory_space=pl.ANY)] * len(late),
        out_specs=[here] * len(outs),
        compiler_params=pltpu.CompilerParams(vmem_limit_bytes=VMEM),
        cost_estimate=pl.CostEstimate(flops=flops, bytes_accessed=moved, transcendentals=0),
        name=name,
    )(place, *ins, *late)


def start(src, dst, sem):
    copy = pltpu.make_async_copy(src, dst, sem)
    copy.start()
    return copy


def columns(weight, place):
    own = weight.shape[1] // 2
    return weight.at[:, pl.ds(pl.multiple_of(place[0] * own, own), own)]


def project(x_ref, half, weight, out, place):
    seqs, rows, width = x_ref.shape
    lanes = 2 * HEAD
    got = jnp.dot(
        x_ref[...].reshape(seqs * rows, width), weight[...], preferred_element_type=F32
    ).astype(BF16)
    for s in range(seqs):
        at = (half * seqs + s) * lanes
        for p in range(out.shape[0]):
            out[p, :, at : at + lanes] = got[s * rows : (s + 1) * rows, p * lanes : (p + 1) * lanes]


def project_heads(x_ref, half, weights, out, place):
    seqs, rows, width = x_ref.shape
    lanes, some = 2 * HEAD, seqs // 2
    group = rows // PARTS
    sides = [
        jnp.dot(
            x_ref[i * some : (i + 1) * some].reshape(some * rows, width),
            weights[i],
            preferred_element_type=F32,
        ).astype(BF16)
        for i in range(2)
    ]
    first = lax.broadcasted_iota(jnp.int32, (rows, lanes), 1) < HEAD
    for s in range(some):
        at = (half * some + s) * lanes
        for p in range(out.shape[0] // 2):
            one, two = (a[s * rows : (s + 1) * rows, p * lanes : (p + 1) * lanes] for a in sides)
            for h in range(2):
                part = jnp.where(first, two, one) if h else jnp.where(first, one, two)
                if len(out.shape) == 3:
                    out[2 * p + h, :, at : at + lanes] = part
                    continue
                for a in range(PARTS):
                    out[2 * p + h, rel(a - place[1]), :, at : at + lanes] = part[
                        a * group : (a + 1) * group
                    ]


def write_logits(queries, keys, outs):
    group = outs[0].shape[2] // 2
    for head in range(keys[0].shape[0]):
        k = jnp.concatenate([ref[head] for ref in keys], axis=0)
        q = jnp.concatenate(
            [
                jnp.concatenate([ref[head].reshape(PARTS * group, -1) for ref in refs], axis=-1)
                for refs in queries
            ],
            axis=0,
        )
        got = lax.dot_general(q, k, (((1,), (1,)), ((), ())), preferred_element_type=F32)
        at = head % 2 * group
        for i in range(len(queries)):
            for d, out in enumerate(outs):
                out[i, head // 2, at : at + group] = got[
                    (i * PARTS + d) * group : (i * PARTS + d + 1) * group
                ].astype(BF16)


def wait_all(copies):
    for copy in copies:
        copy.wait()


def own_body(place, x0, x1, wq, wk, wv, oq, ok, ov, oqw, okw, bx, bw, bq, bk, bv, bs, ins, outs):
    loads = [start(x, bx.at[i], ins.at[i]) for i, x in enumerate((x0, x1))]
    loads += [start(columns(w, place), bw.at[i], ins.at[2 + i]) for i, w in enumerate((wq, wk, wv))]
    lanes = 2 * HEAD
    stores = []
    for i, out in enumerate((oqw, okw)):
        loads[2 + i].wait()
        bs[i, 0] = bw[i]
        for p in range(bw.shape[2] // lanes):
            at = slice(p * lanes, (p + 1) * lanes)
            bs[i, 1, :, at] = pltpu.roll(bw[i, :, at].astype(F32), HEAD, 1).astype(BF16)
        stores.append(start(bs.at[i], out, outs.at[3 + i]))
    for load in loads[:2]:
        load.wait()
    for i, (out, held) in enumerate(((oq, bq), (ok, bk))):
        for half in range(2):
            project_heads(bx.at[half], half, bs.at[i], held, place)
        stores.append(start(held, out, outs.at[i]))
    loads[4].wait()
    for half in range(2):
        project(bx.at[half], half, bw.at[2], bv, place)
    stores.append(start(bv, ov, outs.at[2]))
    wait_all(stores)


def near_body(place, first, second, partner, wq, wk, qa, k1, k2):
    project_heads(first, 0, wk, k1, place)
    project_heads(second, 0, wk, k2, place)
    project_heads(partner, 0, wq, qa, place)


def near_keys_body(place, a1, a2, first, second, wk, k1, k2):
    half = a1.shape[2]
    for a, x, k in ((a1, first, k1), (a2, second, k2)):
        k[:, :, :half] = a[...]
        project_heads(x, 1, wk, k, place)


def near_logits_body(place, q0, qa, k0, k1, k2, partner, wq, qb, *outs):
    project_heads(partner, 0, wq, qb, place)
    write_logits([[q0], [qa, qb]], [k0, k1, k2], outs)


def far_logits_body(place, q0, qa, qb, k, *outs):
    write_logits([[q0], [qa, qb]], [k], outs)


def values_body(place, *refs):
    *xs, weight = refs[: len(refs) * 2 // 3 + 1]
    for i, out in enumerate(refs[len(xs) + 1 :]):
        for half in range(2):
            project(xs[2 * i + half], half, columns(weight, place), out, place)


def near_values_body(place, x0, x1, x2, x3, z_first, weight, both, second):
    for half, x in enumerate((x0, x1)):
        project(x, half, columns(weight, place), both.at[0], place)
    for half, x in enumerate((x2, x3)):
        project(x, half, columns(weight, place), second, place)
    both[1] = z_first[...]


def gather_body(place, own, both, second, far, z_own, z_second, out):
    blocks = (own, both.at[0], second, far.at[0], z_own, both.at[1], z_second, far.at[1])
    rows = own.shape[1]
    for i, ref in enumerate(blocks):
        out[:, i * rows : (i + 1) * rows, :] = ref[...]


def add_body(count, place, *refs):
    out, parts = refs[-1], refs[:-1]
    z_lo = place[3]
    sums = []
    for n in range(0, len(parts), count):
        total = parts[n][...].astype(F32)
        for ref in parts[n + 1 : n + count]:
            total += ref[...].astype(F32)
        sums.append(total)
    total = jnp.concatenate(sums, axis=-1).astype(BF16)
    share = out.shape[2]
    for i in range(2):
        for z in range(PARTS):
            out[z, i ^ z_lo] = total[i, z * share : (z + 1) * share]


def add_parts(place, groups):
    parts = [a for g in groups for a in g]
    rows = parts[0].shape[1]
    cols = sum(g[0].shape[2] for g in groups)
    return local(
        functools.partial(add_body, PARTS),
        place,
        parts,
        [jax.ShapeDtypeStruct((PARTS, 2, rows // PARTS, cols), BF16)],
        sum(a.size for a in parts),
        "add_over_y",
    )[0]


def softmax_body(scale, place, parts, *refs):
    out = refs[len(refs) // 2]
    z_lo = place[3]
    sides = []
    for side in (z_lo, 1 - z_lo):
        total = parts[0, side].astype(F32)
        for z in range(1, PARTS):
            total += parts[z, side].astype(F32)
        sides.append(total)
    scaled = jnp.concatenate(sides, axis=-1) * scale
    expo = jnp.exp(scaled - jnp.max(scaled, axis=-1, keepdims=True))
    out[...] = (expo / jnp.sum(expo, axis=-1, keepdims=True)).astype(BF16)


def softmax(place, parts, scale, others):
    shape = (parts.shape[2], 2 * parts.shape[3])
    free = [pl.BlockSpec(memory_space=pl.ANY)] * len(others)
    here = pl.BlockSpec(memory_space=pltpu.VMEM)
    return pl.pallas_call(
        functools.partial(softmax_body, scale),
        out_shape=[jax.ShapeDtypeStruct(shape, BF16)]
        + [jax.ShapeDtypeStruct(a.shape, a.dtype) for a in others],
        in_specs=[pl.BlockSpec(memory_space=pltpu.SMEM), here, *free],
        out_specs=[here, *free],
        input_output_aliases={2 + i: 1 + i for i in range(len(others))},
        compiler_params=pltpu.CompilerParams(vmem_limit_bytes=VMEM),
        cost_estimate=pl.CostEstimate(
            flops=parts.size * 8, bytes_accessed=parts.size * 4, transcendentals=parts.size // 4
        ),
        name="softmax",
    )(place, parts, *others)


def order_body(place, *refs):
    out, parts = refs[-1], refs[:-1]
    for d, ref in enumerate(parts):
        out[rel(place[2] - d)] = ref[...]


def order(place, parts):
    shape = (PARTS, *parts[0].shape)
    return call(
        order_body,
        place,
        parts,
        [whole(a.shape) for a in parts],
        [jax.ShapeDtypeStruct(shape, BF16)],
        [whole(shape)],
        (1,),
        0,
        "order",
    )[0]


def mix_body(place, *refs):
    probs, values, outs = refs[:PARTS], refs[PARTS], refs[-2:]
    y = place[1]
    pairs, half, _ = probs[0].shape
    group = half // 2
    lanes = 2 * HEAD
    seqs = outs[0].shape[0]
    first = lax.broadcasted_iota(jnp.int32, (group, lanes), 1) < HEAD
    for pair in range(pairs):
        p = jnp.concatenate([ref[pair] for ref in probs], axis=0)
        got = jnp.dot(p, values[pair], preferred_element_type=F32)
        for d in range(PARTS):
            at = pl.multiple_of(rel(y - d) * group, group)
            for s in range(2 * seqs):
                one, two = (
                    got[(2 * d + h) * group : (2 * d + h + 1) * group, s * lanes : (s + 1) * lanes]
                    for h in range(2)
                )
                outs[s // seqs][
                    s % seqs, pl.ds(at, group), pair * lanes : (pair + 1) * lanes
                ] = jnp.where(first, one, two).astype(BF16)


def mix(place, probs, values, seqs):
    pairs, half, cols = probs[0].shape
    rows = PARTS * half // 2
    return local(
        mix_body,
        place,
        [*probs, values],
        [jax.ShapeDtypeStruct((seqs, rows, pairs * 2 * HEAD), BF16)] * 2,
        2 * pairs * PARTS * half * cols * values.shape[2],
        "mix",
    )


def finish_body(mine, theirs, weight_mine, weight_theirs, out):
    seqs, rows, own = mine.shape
    got = jnp.dot(mine[...].reshape(seqs * rows, own), weight_mine[...], preferred_element_type=F32)
    got += jnp.dot(
        theirs[...].reshape(seqs * rows, own), weight_theirs[...], preferred_element_type=F32
    )
    out[...] = got.astype(BF16).reshape(out.shape)


def finish(mine, theirs, weight_mine, weight_theirs):
    seqs, rows, own = mine.shape
    width = weight_mine.shape[1]
    part = seqs // 2
    return pl.pallas_call(
        finish_body,
        out_shape=jax.ShapeDtypeStruct((seqs, rows, width), BF16),
        grid=(seqs // part,),
        in_specs=[pl.BlockSpec((part, rows, own), lambda r: (r, 0, 0))] * 2
        + [pl.BlockSpec((own, width), lambda r: (0, 0))] * 2,
        out_specs=pl.BlockSpec((part, rows, width), lambda r: (r, 0, 0)),
        compiler_params=pltpu.CompilerParams(vmem_limit_bytes=VMEM),
        cost_estimate=pl.CostEstimate(
            flops=2 * seqs * rows * width * width,
            bytes_accessed=4 * seqs * rows * width + 2 * width * width,
            transcendentals=0,
        ),
        name="finish",
    )(mine, theirs, weight_mine, weight_theirs)


def ring_table(axis_of):
    return [
        (c * SIZE["x"] + i, c * SIZE["x"] + (i + (1 if c == axis_of else -1)) % SIZE["x"])
        for c in range(2)
        for i in range(SIZE["x"])
    ]


def send_x(arr, way):
    return lax.ppermute(arr, ("core", "x"), ring_table(way))


def send_y(arr, way):
    table = [
        (i * 2 + c, (i + (1 if c == way else -1)) % PARTS * 2 + c) for i in range(PARTS) for c in range(2)
    ]
    return lax.ppermute(arr, ("y", "core"), table)


def per_device(data, query_matrix, key_matrix, value_matrix, output_matrix):
    seqs, rows, width = data.shape
    place = jnp.stack([lax.axis_index(a) for a in ("core", "y", "z_hi", "z_lo")])
    place = place.astype(jnp.int32)

    core = lax.axis_index("core")
    half = width // 2

    def swap(arr):
        return shift(arr, "core", 1)

    output_mine, output_theirs = (
        lax.dynamic_slice_in_dim(output_matrix, c * half, half, 0) for c in (core, 1 - core)
    )

    pairs, span, group = HEADS // 4, 4 * seqs * HEAD, rows // PARTS
    heads, v_shape = 2 * pairs, (pairs, rows, span)
    q_shape, k_shape = (heads, PARTS, group, span // 2), (heads, rows, span // 2)
    qa_shape, ka_shape = (*q_shape[:-1], span // 4), (*k_shape[:-1], span // 4)
    w_shape = (2, width, half)
    dma = pltpu.SemaphoreType.DMA

    def logits_shape(n):
        return jax.ShapeDtypeStruct((2, pairs, 2 * group, n * rows), BF16)

    def bf(*shape):
        return pltpu.VMEM(shape, BF16)

    first, second = send_x(data, 0), send_x(data, 1)
    partner = shift(data, "z_lo", 1)
    queries, keys, values, query_pair, key_pair = manual(
        own_body,
        place,
        [data, swap(data), query_matrix, key_matrix, value_matrix],
        [jax.ShapeDtypeStruct(s, BF16) for s in (q_shape, k_shape, v_shape, w_shape, w_shape)],
        [bf(2, *data.shape), bf(3, width, half), bf(*q_shape), bf(*k_shape), bf(*v_shape)]
        + [bf(2, *w_shape), dma((5,)), dma((5,))],
        12 * seqs * rows * width * half,
        "own",
    )
    first, second, partner = (tie([a], queries)[0] for a in (first, second, partner))
    near = [(first, swap(second)), (second, swap(first))]
    partner2 = (partner, swap(partner))
    def of(*shapes):
        return [jax.ShapeDtypeStruct(s, BF16) for s in shapes]

    work = 4 * seqs * rows * width * half
    qa, ka1, ka2 = local(
        near_body,
        place,
        [first, second, partner, query_pair, key_pair],
        of(qa_shape, ka_shape, ka_shape),
        3 * work // 2,
        "near",
    )
    k1, k2 = local(
        near_keys_body,
        place,
        [ka1, ka2, near[0][1], near[1][1], key_pair],
        of(k_shape, k_shape),
        work,
        "near_keys",
    )
    far_keys = send_x(k1, 0)
    qb, *near_logits = local(
        near_logits_body,
        place,
        [queries, qa, keys, k1, k2, partner2[1], query_pair],
        of(qa_shape) + [logits_shape(3)] * PARTS,
        2 * work,
        "near_logits",
    )
    (z_own,) = local(
        values_body,
        place,
        [*partner2, value_matrix],
        of(v_shape),
        work,
        "values_partner",
        [qb],
    )
    z_first, z_second = send_x(z_own, 0), send_x(z_own, 1)
    far_logits = local(
        far_logits_body,
        place,
        [queries, qa, qb, far_keys],
        [logits_shape(1)] * PARTS,
        work // 2,
        "far_logits",
        [z_own],
    )
    def over_y(parts, split):
        parts = [a.reshape(2, -1, a.shape[-1]) for a in parts]
        opposite = send_y(send_y(parts[2], 0), 0) if split else shift(parts[2], "y", 2)
        return [parts[0], shift(parts[1], "y", 1), opposite, shift(parts[3], "y", 3)]

    groups = [over_y(near_logits, True), over_y(far_logits, False)]
    sent = add_parts(place, groups)
    both_values, second_values = local(
        near_values_body,
        place,
        [*near[0], *near[1], z_first, value_matrix],
        of((2, *v_shape), v_shape),
        2 * work,
        "values_near",
        [sent],
    )
    sent = sent.reshape(2 * PARTS, *sent.shape[2:])
    got = lax.all_to_all(sent, ("z_hi", "z_lo"), 0, 0, tiled=True)
    got = got.reshape(PARTS, 2, *got.shape[1:])
    all_rows = seqs * lax.axis_size(("z_hi", "y", "core"))
    scale = HEAD ** (-0.5) * all_rows ** (-0.5)
    probs, z_second, both_values = softmax(place, got, scale, [z_second, both_values])
    far_values = send_x(both_values, 0)
    probs = order(place, [probs] + [shift(probs, "z_hi", d) for d in range(1, PARTS)])
    probs = probs.reshape(pairs, 2 * group, probs.shape[-1])
    parts = [values, both_values, second_values, far_values, z_own, z_second]
    (values,) = local(gather_body, place, parts, of((pairs, 8 * rows, span)), 0, "gather_values")
    probs = [probs] + [shift(probs, "y", d) for d in range(1, PARTS)]
    mine, theirs = mix(place, probs, values, seqs)
    return finish(mine, swap(theirs), output_mine, output_theirs)


def solution(mesh):
    fine = Mesh(mesh.devices.reshape(SIZES), AXES)
    spec = P(("z_hi", "y", "core"), ("x", "z_lo"), None)
    return jax.shard_map(
        per_device,
        mesh=fine,
        in_specs=(spec, P(), P(), P(), P()),
        out_specs=spec,
        check_vma=False,
    )
```
